32 devices in a mesh: pool: 2 (over y), tgt: 16 (over z, x, core).
Axes of the slice: x: 2, y: 2, z: 4, core: 2. Of those that a mesh axis runs over, the one named last changes fastest.
Arguments:
- pool_table: bfloat16 [8192, 4096], P('pool', 'tgt'), may hold values from -6 to 6
- pool_index: int32 [2048], P('pool'), may hold values from 0 to 8191, as said below
- target_features: bfloat16 [2048, 4096], P('pool', 'tgt'), may hold values from -6 to 6
- posterior_factor: bfloat16 [4096, 4096], P('tgt'), as said below
Outputs:
- scores: float32 [2048], P('pool')
The draws below stay inside these ranges and needn't reach their ends.
Inputs may be any that keep to these rules, and one draw needn't show every extreme that they name: `pool_index`: pool row r names a row of the table block [(r // 1024) * 4096, (r // 1024 + 1) * 4096); the first row of each block of 1024 pool rows names its table block's first row, and the last names the block's last row; rows may repeat. `posterior_factor`: lower triangular with a positive diagonal.
All inputs are finite; a program needn't handle non-finite values.
Results may differ from the reference program's by a relative error of at most 0.004.
Values may be sent and summed in bfloat16 or wider, within the bound.
No kernel may reach another device: no remote copies, remote signals or barrier semaphores. Data moves between devices by JAX's collectives and lax.ppermute only.
A program may use at most 128 MiB of HBM per device.

```python
import jax
import jax.numpy as jnp
from jax import lax

H = 4096
POOL_DEV = 1024
TABLE_DEV = 4096
POOL = 2048
TARGETS = 2048
TABLE = 8192
N_POOL = 2
N_TGT = 16


def shared_targets(key):
    key_base, key_pick = jax.random.split(key)
    base = jnp.clip(jax.random.normal(key_base, (TARGETS, H), jnp.float32), -5.0, 5.0)
    picked = jax.random.randint(key_pick, (TABLE,), 0, TARGETS, dtype=jnp.int32)
    return (base, picked)


def draw_target_features(key, part):
    base, picked = shared_targets(key)
    return jnp.clip(base, -6.0, 6.0).astype(jnp.bfloat16)


def draw_pool_table(key, part):
    base, picked = shared_targets(key)
    key = jax.random.fold_in(key, 37)
    key_share, key_noise = jax.random.split(key, 2)
    share = jax.random.uniform(key_share, (TABLE, 1), jnp.float32, 0.05, 0.9)
    noise = jnp.clip(jax.random.normal(key_noise, (TABLE, H), jnp.float32), -5.0, 5.0)
    rows = jnp.sqrt(share) * base[picked] + jnp.sqrt(1.0 - share) * noise
    return jnp.clip(rows, -6.0, 6.0).astype(jnp.bfloat16)


def draw_pool_index(key, part):
    key = jax.random.fold_in(key, 11)
    rows = jnp.arange(POOL, dtype=jnp.int32)
    block = rows // POOL_DEV
    offset = jax.random.randint(key, (POOL,), 0, TABLE_DEV, dtype=jnp.int32)
    offset = jnp.where(rows % POOL_DEV == 0, 0, offset)
    offset = jnp.where(rows % POOL_DEV == POOL_DEV - 1, TABLE_DEV - 1, offset)
    return (block * TABLE_DEV + offset).astype(jnp.int32)


def draw_posterior_factor(key, part):
    key = jax.random.fold_in(key, 23)
    key_diag, key_off = jax.random.split(key)
    diag_values = jax.random.uniform(key_diag, (H,), jnp.float32, 0.5, 1.5)
    lower = jax.random.normal(key_off, (H, H), jnp.float32) * (0.6 / H ** 0.5)
    factor = jnp.tril(lower, -1) + jnp.diag(diag_values)
    return factor.astype(jnp.bfloat16)


def setup_inputs(seed: int = 0) -> dict:
    key_of = jax.random.split(jax.random.key(seed), 5)
    return {
        "pool_table": draw_pool_table(jax.random.fold_in(key_of[4], 71), 0),
        "pool_index": draw_pool_index(jax.random.fold_in(key_of[4], 71), 0),
        "target_features": draw_target_features(jax.random.fold_in(key_of[4], 71), 0),
        "posterior_factor": draw_posterior_factor(jax.random.fold_in(key_of[4], 71), 0),
    }


def whiten(features, factor):
    width = H // N_TGT
    blocks = features.reshape(features.shape[0], N_TGT, width).transpose(1, 0, 2)
    factor_blocks = factor.reshape(N_TGT, width, H)

    def add_block(total, pair):
        partial_sum = jnp.dot(pair[0], pair[1], preferred_element_type=jnp.float32)
        partial_sum = lax.optimization_barrier(partial_sum.astype(jnp.bfloat16)).astype(jnp.float32)
        return total + partial_sum, None

    total, unused = lax.scan(add_block, jnp.zeros((features.shape[0], H), jnp.float32), (blocks, factor_blocks))
    return total.astype(jnp.bfloat16)


def reference(pool_table, pool_index, target_features, posterior_factor):
    pool_rows = pool_table[pool_index]
    whitened_pool = whiten(pool_rows, posterior_factor)
    whitened_targets = whiten(target_features, posterior_factor)
    target_var = 1.0 + jnp.sum(jnp.square(whitened_targets.astype(jnp.float32)), axis=1)

    def score_block(rows):
        cross = jnp.dot(rows, whitened_targets.T, preferred_element_type=jnp.float32)
        pool_var = 1.0 + jnp.sum(jnp.square(rows.astype(jnp.float32)), axis=1)
        ratio = jnp.square(cross) / (pool_var[:, None] * target_var[None, :])
        return -0.5 * jnp.sum(jnp.log1p(-ratio), axis=1)

    scores = lax.map(score_block, whitened_pool.reshape(N_POOL, POOL_DEV, H))
    return scores.reshape(POOL)
```

```python
import jax
import jax.numpy as jnp
from jax import lax
from jax.sharding import PartitionSpec as P

QUARTERS = 4
CORES = 2
BF = jnp.bfloat16
F32 = jnp.float32


def matmul(a, b):
    return lax.dot_general(a, b, (((1,), (0,)), ((), ())), preferred_element_type=F32)


def matmul_t(a, b):
    return lax.dot_general(a, b, (((1,), (1,)), ((), ())), preferred_element_type=F32)


def token(*arrays):
    width = min(v.shape[-1] for v in arrays)
    rows = [lax.slice_in_dim(v.reshape(-1, v.shape[-1])[:1], 0, width, axis=1) for v in arrays]
    return sum(jnp.minimum(jnp.abs(r.astype(F32)), 0.0) for r in rows)


def behind(value, zeros):
    return value + zeros[:, :value.shape[-1]].astype(value.dtype)


def square_sum(a):
    return jnp.sum(jnp.square(a.astype(F32)), axis=1)


def make_body(n_pool, n_tgt):
    nz = QUARTERS
    nx = n_tgt // (nz * CORES)
    outer = (1, 0, 3, 2)
    middle = (0, 2, 1, 3)
    spread_out = (3, 2, 1, 0)

    def place(z, x, c):
        return (z * nx + x) * CORES + c

    def inner(value, shift, flip):
        pairs = [
            (place(z, x, c), place(z, (x + shift) % nx, c ^ flip))
            for z in range(nz) for x in range(nx) for c in range(CORES)
        ]
        return lax.ppermute(value, "tgt", pairs)

    def along_z(value, to):
        pairs = [
            (place(z, x, c), place(to[z], x, c)) for z in range(nz) for x in range(nx) for c in range(CORES)
        ]
        return lax.ppermute(value, "tgt", pairs)

    def over_pool(value, shift):
        return lax.ppermute(value, "pool", [(p, (p + shift) % n_pool) for p in range(n_pool)])

    def choose(values, z):
        out = jnp.int32(values[0])
        for k in range(1, nz):
            out = jnp.where(z == k, jnp.int32(values[k]), out)
        return out

    def body(pool_table, pool_index, target_features, posterior_factor):
        me = lax.axis_index("tgt")
        core = me % CORES
        x = (me // CORES) % nx
        z = me // (CORES * nx)
        top = z == nz - 1
        width, hidden = posterior_factor.shape
        quarter = hidden // nz

        local_index = pool_index - lax.axis_index("pool") * pool_table.shape[0]
        pool_rows = jnp.take(pool_table, local_index, axis=0)
        count = pool_rows.shape[0] // (nx * CORES)
        count_t = target_features.shape[0] // (nx * CORES)

        rows = jnp.concatenate([
            target_features.reshape(nx, CORES, count_t, width), pool_rows.reshape(nx, CORES, count, width)
        ], axis=2)
        n_rows = count + count_t

        def rows_of(s, f):
            return lax.dynamic_slice(rows, (lax.rem(x + s, nx), core ^ f, 0, 0), (1, 1, n_rows, width))[0, 0]

        def factor_own(choice):
            return lax.dynamic_slice_in_dim(posterior_factor, choose(choice, z) * quarter, quarter, 1)

        def factor_x(own):
            return [inner(own, s, 0) for s in range(1, nx)]

        def partial(pieces):
            total = None
            for f, l in zip(features, pieces):
                term = matmul(f, l)
                total = term if total is None else total + term
            return total

        def factor_flip(same):
            return [inner(v, 0, 1) for v in same]

        order = [(s, 0) for s in range(nx)] + [(s, 1) for s in range(nx)]

        own1 = factor_own([0, 1, 2, 1])
        same1 = [own1] + factor_x(own1)

        done = token(*same1[1:])
        features = [inner(behind(rows_of(s, f), done), s, f) if s or f else rows_of(0, 0) for s, f in order]
        first = partial(same1 + factor_flip(same1))

        start = token(first)
        step1 = along_z(first.astype(BF), outer)
        step2 = along_z(first.astype(BF), middle)
        own2 = behind(factor_own([0, 0, 0, 0]), start)
        own3 = behind(factor_own([1, 1, 1, 2]), start)
        flip2, flip3 = inner(own2, 0, 1), inner(own3, 0, 1)
        moved2, moved3 = factor_x(own2), factor_x(own3)
        done = token(step1, step2, flip2, flip3, *moved2, *moved3)
        moved2, moved3 = [behind(v, done) for v in moved2], [behind(v, done) for v in moved3]
        second = partial([own2] + moved2 + [flip2] + factor_flip(moved2))
        third = partial([own3] + moved3 + [flip3] + factor_flip(moved3))

        start = token(second, third) + done
        step3 = along_z(behind(second, start).astype(BF), outer)
        step4 = along_z((behind(second, start) + step1.astype(F32)).astype(BF), middle)
        white_a = (third + step1.astype(F32) + jnp.where(top, 0.0, step2.astype(F32)) + start).astype(BF)
        own4 = behind(factor_own([3, 3, 3, 3]), start)
        flip4, moved4 = inner(own4, 0, 1), factor_x(own4)
        t_a, p_a = white_a[:count_t], white_a[count_t:]
        t_flip_a = inner(t_a, 0, 1)
        t_moved_a = [inner(t_a, s, 0) for s in range(1, nx)]
        p_moved_a = [over_pool(p_a, s) for s in range(1, n_pool)]
        done = token(step3, step4, flip4, *moved4, t_flip_a, *t_moved_a, *p_moved_a)

        moved4 = [behind(v, done) for v in moved4]
        fourth = partial([own4] + moved4 + [flip4] + factor_flip(moved4))
        t_moved_a = [behind(v, done) for v in t_moved_a]
        white_b = (jnp.where(top, fourth, second + step3.astype(F32) + step4.astype(F32)) + done).astype(BF)
        t_b, p_b = white_b[:count_t], white_b[count_t:]
        t_moved_b = [inner(t_b, s, 0) for s in range(1, nx)]
        p_moved_b = [over_pool(p_b, s) for s in range(1, n_pool)]
        t_flip_b = inner(t_b, 0, 1)

        def spread(t, t_moved, t_flip, p, p_moved):
            low = jnp.concatenate([t] + t_moved, axis=0)
            high = jnp.concatenate([t_flip] + [inner(v, 0, 1) for v in t_moved], axis=0)
            return jnp.where(top, high, low), jnp.where(top, low, high), jnp.concatenate([p] + p_moved, axis=0)

        keep_a, give_a, p_a = spread(t_a, t_moved_a, t_flip_a, p_a, p_moved_a)
        keep_b, give_b, p_b = spread(t_b, t_moved_b, t_flip_b, p_b, p_moved_b)

        given = along_z(matmul_t(give_a, p_a) + matmul_t(give_b, p_b), outer)
        p_squares = square_sum(p_a) + square_sum(p_b)
        n_keep = keep_a.shape[0]
        squares = along_z(jnp.concatenate([square_sum(give_a) + square_sum(give_b), p_squares]), outer)
        target_var = 1.0 + (square_sum(keep_a) + square_sum(keep_b) + squares[:n_keep])
        pool_var = 1.0 + (p_squares + squares[n_keep:])
        cross = matmul_t(keep_a, p_a) + matmul_t(keep_b, p_b) + given
        ratio = jnp.square(cross) / (target_var[:, None] * pool_var[None, :])
        sums = -0.5 * jnp.sum(jnp.log1p(-ratio), axis=0)

        sums = sums + along_z(sums, outer)
        own = sums[:count]
        for s in range(1, n_pool):
            own = own + over_pool(sums[s * count:(s + 1) * count], -s)
        flipped = inner(own, 0, 1)
        both = jnp.where(core == 0, jnp.concatenate([own, flipped]), jnp.concatenate([flipped, own]))
        parts = jnp.stack([both] + [inner(both, s, 0) for s in range(1, nx)])
        if nx == 2:
            scores = jnp.where(x == 0, parts.reshape(-1), parts[::-1].reshape(-1))
        else:
            scores = jnp.take(parts, (x - jnp.arange(nx)) % nx, axis=0).reshape(-1)
        return jnp.where(z >= nz - 2, scores, along_z(scores, spread_out))

    return body


def solution(mesh):
    in_specs = (P("pool", "tgt"), P("pool"), P("pool", "tgt"), P("tgt", None))
    out_specs = P("pool")
    body = make_body(mesh.shape["pool"], mesh.shape["tgt"])
    return jax.shard_map(body, mesh=mesh, in_specs=in_specs, out_specs=out_specs, check_vma=False)
```

```python
import jax
import jax.numpy as jnp
from jax import lax
from jax.sharding import PartitionSpec as P

QUARTERS = 4
CORES = 2
BF = jnp.bfloat16
F32 = jnp.float32


def matmul(a, b):
    return lax.dot_general(a, b, (((1,), (0,)), ((), ())), preferred_element_type=F32)


def matmul_t(a, b):
    return lax.dot_general(a, b, (((1,), (1,)), ((), ())), preferred_element_type=F32)


def token(*arrays):
    width = min(v.shape[-1] for v in arrays)
    rows = [lax.slice_in_dim(v.reshape(-1, v.shape[-1])[:1], 0, width, axis=1) for v in arrays]
    return sum(jnp.minimum(jnp.abs(r.astype(F32)), 0.0) for r in rows)


def behind(value, zeros):
    zeros = zeros if zeros.shape[-1] == 1 else zeros[:, :value.shape[-1]]
    return value + zeros.astype(value.dtype)


def square_sum(a):
    return jnp.sum(jnp.square(a.astype(F32)), axis=1)


def make_body(n_pool, n_tgt):
    nz = QUARTERS
    nx = n_tgt // (nz * CORES)
    outer = (1, 0, 3, 2)
    middle = (0, 2, 1, 3)
    mirror = (3, 2, 1, 0)

    def place(z, x, c):
        return (z * nx + x) * CORES + c

    def inner(value, shift, flip):
        pairs = [
            (place(z, x, c), place(z, (x + shift) % nx, c ^ flip))
            for z in range(nz) for x in range(nx) for c in range(CORES)
        ]
        return lax.ppermute(value, "tgt", pairs)

    def along_z(value, to):
        pairs = [
            (place(z, x, c), place(to[z], x, c)) for z in range(nz) for x in range(nx) for c in range(CORES)
        ]
        return lax.ppermute(value, "tgt", pairs)

    def over_pool(value, shift, flip=0, to=None):
        to = to or range(nz)
        pairs = [
            (p * n_tgt + place(z, x, c), ((p + shift) % n_pool) * n_tgt + place(to[z], x, c ^ flip))
            for p in range(n_pool) for z in range(nz) for x in range(nx) for c in range(CORES)
        ]
        return lax.ppermute(value, ("pool", "tgt"), pairs)

    def in_order(pieces, index):
        n = len(pieces)
        if n == 2:
            low = index == 0
            return jnp.concatenate([jnp.where(low, pieces[0], pieces[1]), jnp.where(low, pieces[1], pieces[0])], axis=0)
        stacked = jnp.take(jnp.stack(pieces), (index - jnp.arange(n)) % n, axis=0)
        return stacked.reshape((-1,) + stacked.shape[2:])

    def choose(values, z):
        out = jnp.int32(values[0])
        for k in range(1, nz):
            out = jnp.where(z == k, jnp.int32(values[k]), out)
        return out

    def body(pool_table, pool_index, target_features, posterior_factor):
        me = lax.axis_index("tgt")
        core = me % CORES
        x = (me // CORES) % nx
        z = me // (CORES * nx)
        top = z == nz - 1
        width, hidden = posterior_factor.shape
        quarter = hidden // nz

        local_index = pool_index - lax.axis_index("pool") * pool_table.shape[0]
        pool_rows = pool_table.at[local_index].get(mode="promise_in_bounds")
        count = pool_rows.shape[0] // (nx * CORES)
        count_t = target_features.shape[0] // (nx * CORES)

        rows = jnp.concatenate([
            target_features.reshape(nx, CORES, count_t, width), pool_rows.reshape(nx, CORES, count, width)
        ], axis=2)
        n_rows = count + count_t

        def rows_of(s, f):
            return lax.dynamic_slice(rows, (lax.rem(x + s, nx), core ^ f, 0, 0), (1, 1, n_rows, width))[0, 0]

        def factor_own(choice):
            return lax.dynamic_slice_in_dim(posterior_factor, choose(choice, z) * quarter, quarter, 1)

        def factor_x(own):
            return [inner(own, s, 0) for s in range(1, nx)]

        def partial(pieces):
            total = None
            for f, l in zip(features, pieces):
                term = matmul(f, l)
                total = term if total is None else total + term
            return total

        def factor_flip(same):
            return [inner(v, 0, 1) for v in same]

        order = [(s, 0) for s in range(nx)] + [(s, 1) for s in range(nx)]

        pool = lax.axis_index("pool")
        part_rows = width // n_pool
        own1 = factor_own([0, 1, 2, 1])
        mine1 = lax.dynamic_slice_in_dim(own1, pool * part_rows, part_rows, 0)
        parts1 = [inner(mine1, s, 0) for s in range(1, nx)]

        done = token(*parts1)
        features = [inner(behind(rows_of(s, f), done), s, f) if s or f else rows_of(0, 0) for s, f in order]
        flip1 = inner(own1, 0, 1)
        near1, far1 = [], []
        for v in parts1:
            v = behind(v, done)
            near1.append([v] + [over_pool(v, r) for r in range(1, n_pool)])
            far1.append([inner(v, 0, 1)] + [over_pool(v, r, 1) for r in range(1, n_pool)])
        done = token(*[v for (s, _), v in zip(order, features) if s])
        near1, far1 = [[in_order([behind(v, done[:, :1]) for v in u], pool) for u in w] for w in (near1, far1)]
        first = partial([own1] + near1 + [flip1] + far1).astype(BF)

        start = token(first)
        step1 = along_z(first, outer)
        step2 = along_z(first, middle)
        own2 = behind(factor_own([0, 0, 0, 0]), start)
        own3 = behind(factor_own([1, 1, 1, 2]), start)
        flip2, flip3 = inner(own2, 0, 1), inner(own3, 0, 1)
        moved2, moved3 = factor_x(own2), factor_x(own3)
        done = token(step1, step2, flip2, flip3, *moved2, *moved3)
        moved2, moved3 = [behind(v, done) for v in moved2], [behind(v, done) for v in moved3]
        second = partial([own2] + moved2 + [flip2] + factor_flip(moved2))
        third = partial([own3] + moved3 + [flip3] + factor_flip(moved3))

        start = token(second, third) + done
        step3 = along_z(behind(second, start).astype(BF), outer)
        step4 = along_z((behind(second, start) + step1.astype(F32)).astype(BF), middle)
        white_a = (third + step1.astype(F32) + jnp.where(top, 0.0, step2.astype(F32)) + start).astype(BF)
        own4 = behind(factor_own([3, 3, 3, 3]), start)
        flip4, moved4 = inner(own4, 0, 1), factor_x(own4)
        t_a, p_a = white_a[:count_t], white_a[count_t:]
        t_flip_a = inner(t_a, 0, 1)
        t_moved_a = [inner(t_a, s, 0) for s in range(1, nx)]
        p_moved_a = [over_pool(p_a, s) for s in range(1, n_pool)]
        done = token(step3, step4, flip4, *moved4, t_flip_a, *t_moved_a, *p_moved_a)

        moved4 = [behind(v, done) for v in moved4]
        fourth = partial([own4] + moved4 + [flip4] + factor_flip(moved4))
        t_moved_a = [behind(v, done) for v in t_moved_a]
        white_b = (jnp.where(top, fourth, second + step3.astype(F32) + step4.astype(F32)) + done).astype(BF)
        t_b, p_b = white_b[:count_t], white_b[count_t:]
        t_moved_b = [inner(t_b, s, 0) for s in range(1, nx)]
        p_moved_b = [over_pool(p_b, s) for s in range(1, n_pool)]
        t_flip_b = inner(t_b, 0, 1)

        def groups(t, t_moved, t_flip):
            far, far_flip = jnp.concatenate(t_moved, axis=0), jnp.concatenate([inner(v, 0, 1) for v in t_moved], axis=0)
            keep = jnp.where(top, t_flip, t), jnp.where(top, far_flip, far)
            give = jnp.where(top, t, t_flip), jnp.where(top, far, far_flip)
            return keep, give

        keep_a, give_a = groups(t_a, t_moved_a, t_flip_a)
        keep_b, give_b = groups(t_b, t_moved_b, t_flip_b)
        p_far_a, p_far_b = jnp.concatenate(p_moved_a, axis=0), jnp.concatenate(p_moved_b, axis=0)
        p_all_a, p_all_b = jnp.concatenate([p_a, p_far_a], axis=0), jnp.concatenate([p_b, p_far_b], axis=0)

        given_near = along_z(matmul_t(give_a[0], p_a) + matmul_t(give_b[0], p_b), outer)
        swapped = token(given_near)[:, :1]
        give_side = behind(matmul_t(give_a[0], p_far_a) + matmul_t(give_b[0], p_far_b), swapped)
        give_far = behind(matmul_t(give_a[1], p_all_a) + matmul_t(give_b[1], p_all_b), swapped)
        if nx == 2:
            given = along_z(jnp.concatenate([give_side, give_far], axis=1), outer)
            given_side, given_far = given[:, :give_side.shape[1]], given[:, give_side.shape[1]:]
        else:
            given_side, given_far = along_z(give_side, outer), along_z(give_far, outer)

        p_squares = square_sum(p_all_a) + square_sum(p_all_b)
        sizes = [p_squares.shape[0], keep_a[0].shape[0], keep_a[1].shape[0]]
        squares = along_z(jnp.concatenate(
            [p_squares] + [square_sum(a) + square_sum(b) for a, b in zip(give_a, give_b)]
        ), outer)
        pool_var = 1.0 + (p_squares + squares[:sizes[0]])

        def log_sums(group, given, offset):
            a, b = keep_a[group], keep_b[group]
            target_var = 1.0 + (square_sum(a) + square_sum(b) + squares[offset:offset + sizes[1 + group]])
            cross = matmul_t(a, p_all_a) + matmul_t(b, p_all_b) + given
            ratio = jnp.square(cross) / (target_var[:, None] * pool_var[None, :])
            return -0.5 * jnp.sum(jnp.log1p(-ratio), axis=0)

        sums = log_sums(0, jnp.concatenate([given_near, given_side], axis=1), sizes[0])
        sums = sums + log_sums(1, given_far, sizes[0] + sizes[1])

        blocks = [sums[s * count:(s + 1) * count] for s in range(n_pool)]
        own = blocks[0] + along_z(blocks[0], outer)
        for s in range(1, n_pool):
            own = own + (over_pool(blocks[s], -s) + over_pool(blocks[s], -s, 0, outer))
        rows = [in_order([own if s == 0 else inner(own, s, 0), inner(own, s, 1)], core) for s in range(nx)]
        scores = in_order(rows, x)
        return jnp.where(z >= nz - 2, scores, along_z(scores, mirror))

    return body


def solution(mesh):
    in_specs = (P("pool", "tgt"), P("pool"), P("pool", "tgt"), P("tgt", None))
    out_specs = P("pool")
    body = make_body(mesh.shape["pool"], mesh.shape["tgt"])
    return jax.shard_map(body, mesh=mesh, in_specs=in_specs, out_specs=out_specs, check_vma=False)
```

```python
import jax
import jax.numpy as jnp
from jax import lax
from jax.sharding import PartitionSpec as P

QUARTERS = 4
CORES = 2
BF = jnp.bfloat16
F32 = jnp.float32


def matmul(a, b):
    return lax.dot_general(a, b, (((1,), (0,)), ((), ())), preferred_element_type=F32)


def matmul_t(a, b):
    return lax.dot_general(a, b, (((1,), (1,)), ((), ())), preferred_element_type=F32)


def token(*arrays):
    width = min(v.shape[-1] for v in arrays)
    rows = [lax.slice_in_dim(v.reshape(-1, v.shape[-1])[:1], 0, width, axis=1) for v in arrays]
    return sum(jnp.minimum(jnp.abs(r.astype(F32)), 0.0) for r in rows)


def fence(swap, middle, others):
    done = lax.optimization_barrier(token(swap))
    done = lax.optimization_barrier(token(middle) + done)
    return token(*others) + done


def behind(value, zeros):
    zeros = zeros if zeros.shape[-1] == 1 else zeros[:, :value.shape[-1]]
    return value + zeros.astype(value.dtype)


def square_sum(a):
    return jnp.sum(jnp.square(a.astype(F32)), axis=1)


def make_body(n_pool, n_tgt):
    nz = QUARTERS
    nx = n_tgt // (nz * CORES)
    outer = (1, 0, 3, 2)
    middle = (0, 2, 1, 3)
    skip = (2, 3, 0, 1)

    def place(z, x, c):
        return (z * nx + x) * CORES + c

    def inner(value, shift, flip):
        pairs = [
            (place(z, x, c), place(z, (x + shift) % nx, c ^ flip))
            for z in range(nz) for x in range(nx) for c in range(CORES)
        ]
        return lax.ppermute(value, "tgt", pairs)

    def along_z(value, to):
        pairs = [
            (place(z, x, c), place(to[z], x, c)) for z in range(nz) for x in range(nx) for c in range(CORES)
        ]
        return lax.ppermute(value, "tgt", pairs)

    def over_pool(value, shift, flip=0, to=None):
        to = to or range(nz)
        pairs = [
            (p * n_tgt + place(z, x, c), ((p + shift) % n_pool) * n_tgt + place(to[z], x, c ^ flip))
            for p in range(n_pool) for z in range(nz) for x in range(nx) for c in range(CORES)
        ]
        return lax.ppermute(value, ("pool", "tgt"), pairs)

    def in_order(pieces, index):
        n = len(pieces)
        if n == 2:
            low = index == 0
            return jnp.concatenate([jnp.where(low, pieces[0], pieces[1]), jnp.where(low, pieces[1], pieces[0])], axis=0)
        stacked = jnp.take(jnp.stack(pieces), (index - jnp.arange(n)) % n, axis=0)
        return stacked.reshape((-1,) + stacked.shape[2:])

    def choose(values, z):
        out = jnp.int32(values[0])
        for k in range(1, nz):
            out = jnp.where(z == k, jnp.int32(values[k]), out)
        return out

    def body(pool_table, pool_index, target_features, posterior_factor):
        me = lax.axis_index("tgt")
        core = me % CORES
        x = (me // CORES) % nx
        z = me // (CORES * nx)
        top = z == nz - 1
        width, hidden = posterior_factor.shape
        quarter = hidden // nz

        local_index = pool_index - lax.axis_index("pool") * pool_table.shape[0]
        pool_rows = pool_table.at[local_index].get(mode="promise_in_bounds")
        count = pool_rows.shape[0] // (nx * CORES)
        count_t = target_features.shape[0] // (nx * CORES)

        rows = jnp.concatenate([
            target_features.reshape(nx, CORES, count_t, width), pool_rows.reshape(nx, CORES, count, width)
        ], axis=2)
        n_rows = count + count_t

        def rows_of(s, f):
            return lax.dynamic_slice(rows, (lax.rem(x + s, nx), core ^ f, 0, 0), (1, 1, n_rows, width))[0, 0]

        def factor_own(choice):
            return lax.dynamic_slice_in_dim(posterior_factor, choose(choice, z) * quarter, quarter, 1)

        def factor_x(own):
            return [inner(own, s, 0) for s in range(1, nx)]

        def partial(pieces):
            total = None
            for f, l in zip(features, pieces):
                term = matmul(f, l)
                total = term if total is None else total + term
            return total

        def factor_flip(same):
            return [inner(v, 0, 1) for v in same]

        order = [(s, 0) for s in range(nx)] + [(s, 1) for s in range(nx)]

        pool = lax.axis_index("pool")
        part_rows = width // n_pool
        own1 = lax.optimization_barrier(factor_own([0, 1, 2, 1]))
        mine1 = lax.dynamic_slice_in_dim(own1, pool * part_rows, part_rows, 0)
        parts1 = [inner(mine1, s, 0) for s in range(1, nx)]

        done = token(*parts1)
        features = [inner(behind(rows_of(s, f), done), s, f) if s or f else rows_of(0, 0) for s, f in order]
        flip1 = inner(own1, 0, 1)
        near1, far1 = [], []
        for v in parts1:
            near1.append([v] + [over_pool(v, r) for r in range(1, n_pool)])
            far1.append([inner(v, 0, 1)] + [over_pool(v, r, 1) for r in range(1, n_pool)])
        done = token(*features[1:nx])
        near1, far1 = [[in_order([behind(v, done[:, :1]) for v in u], pool) for u in w] for w in (near1, far1)]
        first = partial([own1] + near1 + [flip1] + far1).astype(BF)

        start = token(first)
        step1 = along_z(first, outer)
        step2 = along_z(first, middle)
        own2 = behind(factor_own([0, 0, 0, 0]), start)
        own3 = behind(factor_own([1, 1, 1, 2]), start)
        flip2, flip3 = inner(own2, 0, 1), inner(own3, 0, 1)
        moved2, moved3 = factor_x(own2), factor_x(own3)
        done = fence(step1, step2, [flip2, flip3, *moved2, *moved3])
        moved2, moved3 = [behind(v, done) for v in moved2], [behind(v, done) for v in moved3]
        second = partial([own2] + moved2 + [flip2] + factor_flip(moved2))
        third = partial([own3] + moved3 + [flip3] + factor_flip(moved3))

        start = token(second, third) + done
        step3 = along_z(behind(second, start).astype(BF), outer)
        step4 = along_z((behind(second, start) + step1.astype(F32)).astype(BF), middle)
        white_a = (third + step1.astype(F32) + jnp.where(top, 0.0, step2.astype(F32)) + start).astype(BF)
        own4 = behind(factor_own([3, 3, 3, 3]), start)
        flip4, moved4 = inner(own4, 0, 1), factor_x(own4)
        t_a, p_a = white_a[:count_t], white_a[count_t:]
        t_flip_a = inner(t_a, 0, 1)
        t_moved_a = [inner(t_a, s, 0) for s in range(1, nx)]
        p_moved_a = [over_pool(p_a, s) for s in range(1, n_pool)]
        done = fence(step3, step4, [flip4, *moved4, t_flip_a, *t_moved_a, *p_moved_a])

        moved4 = [behind(v, done) for v in moved4]
        fourth = partial([own4] + moved4 + [flip4] + factor_flip(moved4))
        t_moved_a = [behind(v, done) for v in t_moved_a]
        white_b = (jnp.where(top, fourth, second + step3.astype(F32) + step4.astype(F32)) + done).astype(BF)
        t_b, p_b = white_b[:count_t], white_b[count_t:]
        t_moved_b = [inner(t_b, s, 0) for s in range(1, nx)]
        p_moved_b = [over_pool(p_b, s) for s in range(1, n_pool)]
        t_flip_b = inner(t_b, 0, 1)

        def groups(t, t_moved, t_flip):
            far, far_flip = jnp.concatenate(t_moved, axis=0), jnp.concatenate([inner(v, 0, 1) for v in t_moved], axis=0)
            keep = jnp.where(top, t_flip, t), jnp.where(top, far_flip, far)
            give = jnp.where(top, t, t_flip), jnp.where(top, far, far_flip)
            return keep, give

        keep_a, give_a = groups(t_a, t_moved_a, t_flip_a)
        keep_b, give_b = groups(t_b, t_moved_b, t_flip_b)
        p_far_a, p_far_b = jnp.concatenate(p_moved_a, axis=0), jnp.concatenate(p_moved_b, axis=0)
        p_all_a, p_all_b = jnp.concatenate([p_a, p_far_a], axis=0), jnp.concatenate([p_b, p_far_b], axis=0)

        given_near = along_z(matmul_t(give_a[0], p_a) + matmul_t(give_b[0], p_b), outer)
        give_side = behind(matmul_t(give_a[0], p_far_a) + matmul_t(give_b[0], p_far_b), token(given_near)[:, :1] if n_pool > 2 else token(given_near))
        give_far = matmul_t(give_a[1], p_all_a) + matmul_t(give_b[1], p_all_b)
        if nx == 2:
            given = along_z(jnp.concatenate([give_side, give_far], axis=1), outer)
            given_side, given_far = given[:, :give_side.shape[1]], given[:, give_side.shape[1]:]
        else:
            given_side, given_far = along_z(give_side, outer), along_z(give_far, outer)

        p_squares = square_sum(p_all_a) + square_sum(p_all_b)
        sizes = [p_squares.shape[0], keep_a[0].shape[0], keep_a[1].shape[0]]
        squares = along_z(jnp.concatenate(
            [p_squares] + [square_sum(a) + square_sum(b) for a, b in zip(give_a, give_b)]
        ), outer)
        pool_var = 1.0 + (p_squares + squares[:sizes[0]])

        def log_sums(group, given, offset):
            a, b = keep_a[group], keep_b[group]
            target_var = 1.0 + (square_sum(a) + square_sum(b) + squares[offset:offset + sizes[1 + group]])
            cross = matmul_t(a, p_all_a) + matmul_t(b, p_all_b) + given
            ratio = jnp.square(cross) / (target_var[:, None] * pool_var[None, :])
            return -0.5 * jnp.sum(jnp.log1p(-ratio), axis=0)

        sums = log_sums(0, jnp.concatenate([given_near, given_side], axis=1), sizes[0])
        sums = sums + log_sums(1, given_far, sizes[0] + sizes[1])

        blocks = [sums[s * count:(s + 1) * count] for s in range(n_pool)]
        own = blocks[0] + along_z(blocks[0], outer)
        for s in range(1, n_pool):
            own = own + (over_pool(blocks[s], -s) + over_pool(blocks[s], -s, 0, outer))
        rows = [in_order([own if s == 0 else inner(own, s, 0), inner(own, s, 1)], core) for s in range(nx)]
        scores = in_order(rows, x)
        return jnp.where(z >= nz - 2, scores, along_z(scores, skip))

    return body


def solution(mesh):
    in_specs = (P("pool", "tgt"), P("pool"), P("pool", "tgt"), P("tgt", None))
    out_specs = P("pool")
    body = make_body(mesh.shape["pool"], mesh.shape["tgt"])
    return jax.shard_map(body, mesh=mesh, in_specs=in_specs, out_specs=out_specs, check_vma=False)
```

```python
import jax
import jax.numpy as jnp
from jax import lax
from jax.sharding import PartitionSpec as P

QUARTERS = 4
CORES = 2
BF = jnp.bfloat16
F32 = jnp.float32


def matmul(a, b):
    return lax.dot_general(a, b, (((1,), (0,)), ((), ())), preferred_element_type=F32)


def matmul_t(a, b):
    return lax.dot_general(a, b, (((1,), (1,)), ((), ())), preferred_element_type=F32)


def token(*arrays):
    width = min(v.shape[-1] for v in arrays)
    rows = [lax.slice_in_dim(v.reshape(-1, v.shape[-1])[:1], 0, width, axis=1) for v in arrays]
    return sum(jnp.minimum(jnp.abs(r.astype(F32)), 0.0) for r in rows)


def fence(middle, swap, others):
    done = lax.optimization_barrier(token(middle))
    done = lax.optimization_barrier(token(swap) + done)
    return token(*others) + done


def behind(value, zeros):
    zeros = zeros if zeros.shape[-1] == 1 else zeros[:, :value.shape[-1]]
    return value + zeros.astype(value.dtype)


def square_sum(a):
    return jnp.sum(jnp.square(a.astype(F32)), axis=1)


def make_body(n_pool, n_tgt):
    nz = QUARTERS
    nx = n_tgt // (nz * CORES)
    outer = (1, 0, 3, 2)
    middle = (0, 2, 1, 3)
    skip = (2, 3, 0, 1)

    def place(z, x, c):
        return (z * nx + x) * CORES + c

    def inner(value, shift, flip):
        pairs = [
            (place(z, x, c), place(z, (x + shift) % nx, c ^ flip))
            for z in range(nz) for x in range(nx) for c in range(CORES)
        ]
        return lax.ppermute(value, "tgt", pairs)

    def along_z(value, to):
        pairs = [
            (place(z, x, c), place(to[z], x, c)) for z in range(nz) for x in range(nx) for c in range(CORES)
        ]
        return lax.ppermute(value, "tgt", pairs)

    def over_pool(value, shift, flip=0, to=None):
        to = to or range(nz)
        pairs = [
            (p * n_tgt + place(z, x, c), ((p + shift) % n_pool) * n_tgt + place(to[z], x, c ^ flip))
            for p in range(n_pool) for z in range(nz) for x in range(nx) for c in range(CORES)
        ]
        return lax.ppermute(value, ("pool", "tgt"), pairs)

    def in_order(pieces, index):
        n = len(pieces)
        if n == 2:
            low = index == 0
            return jnp.concatenate([jnp.where(low, pieces[0], pieces[1]), jnp.where(low, pieces[1], pieces[0])], axis=0)
        stacked = jnp.take(jnp.stack(pieces), (index - jnp.arange(n)) % n, axis=0)
        return stacked.reshape((-1,) + stacked.shape[2:])

    def choose(values, z):
        out = jnp.int32(values[0])
        for k in range(1, nz):
            out = jnp.where(z == k, jnp.int32(values[k]), out)
        return out

    def body(pool_table, pool_index, target_features, posterior_factor):
        me = lax.axis_index("tgt")
        core = me % CORES
        x = (me // CORES) % nx
        z = me // (CORES * nx)
        top = z == nz - 1
        width, hidden = posterior_factor.shape
        quarter = hidden // nz

        local_index = pool_index - lax.axis_index("pool") * pool_table.shape[0]
        pool_rows = pool_table.at[local_index].get(mode="promise_in_bounds")
        count = pool_rows.shape[0] // (nx * CORES)
        count_t = target_features.shape[0] // (nx * CORES)

        rows = jnp.concatenate([
            target_features.reshape(nx, CORES, count_t, width), pool_rows.reshape(nx, CORES, count, width)
        ], axis=2)
        n_rows = count + count_t

        def rows_of(s, f):
            return lax.dynamic_slice(rows, (lax.rem(x + s, nx), core ^ f, 0, 0), (1, 1, n_rows, width))[0, 0]

        def factor_own(choice):
            return lax.dynamic_slice_in_dim(posterior_factor, choose(choice, z) * quarter, quarter, 1)

        def factor_x(own):
            return [inner(own, s, 0) for s in range(1, nx)]

        def partial(pieces):
            total = None
            for f, l in zip(features, pieces):
                term = matmul(f, l)
                total = term if total is None else total + term
            return total

        def factor_flip(same):
            return [inner(v, 0, 1) for v in same]

        order = [(s, 0) for s in range(nx)] + [(s, 1) for s in range(nx)]

        pool = lax.axis_index("pool")
        part_rows = width // n_pool
        own1 = lax.optimization_barrier(factor_own([0, 1, 2, 1]))
        mine1 = lax.dynamic_slice_in_dim(own1, pool * part_rows, part_rows, 0)
        parts1 = [inner(mine1, s, 0) for s in range(1, nx)]

        done = token(*parts1)
        features = [inner(behind(rows_of(s, f), done), s, f) if s or f else rows_of(0, 0) for s, f in order]
        flip1 = inner(own1, 0, 1)
        near1, far1 = [], []
        for v in parts1:
            near1.append([v] + [over_pool(v, r) for r in range(1, n_pool)])
            far1.append([inner(v, 0, 1)] + [over_pool(v, r, 1) for r in range(1, n_pool)])
        done = token(*features[1:nx])
        crossed = token(*features[nx + 1:])[:, :1]
        joined = lax.optimization_barrier(token(*[v for u in far1 for v in u]) + crossed)
        near1 = [in_order([behind(v, done[:, :1]) for v in u], pool) for u in near1]
        far1 = [in_order([behind(v, joined) for v in u], pool) for u in far1]
        first = partial([own1] + near1 + [flip1] + far1).astype(BF)

        start = token(first)
        step1 = along_z(first, outer)
        step2 = along_z(first, middle)
        own2 = behind(factor_own([0, 0, 0, 0]), start)
        own3 = behind(factor_own([1, 1, 1, 2]), start)
        flip2, flip3 = inner(own2, 0, 1), inner(own3, 0, 1)
        moved2, moved3 = factor_x(own2), factor_x(own3)
        done = fence(step2, step1, [flip2, flip3, *moved2, *moved3])
        moved2, moved3 = [behind(v, done) for v in moved2], [behind(v, done) for v in moved3]
        second = partial([own2] + moved2 + [flip2] + factor_flip(moved2))
        third = partial([own3] + moved3 + [flip3] + factor_flip(moved3))

        start = token(second, third) + done
        step3 = along_z(behind(second, start).astype(BF), outer)
        step4 = along_z((behind(second, start) + step1.astype(F32)).astype(BF), middle)
        white_a = (third + step1.astype(F32) + jnp.where(top, 0.0, step2.astype(F32)) + start).astype(BF)
        own4 = behind(factor_own([3, 3, 3, 3]), start)
        flip4, moved4 = inner(own4, 0, 1), factor_x(own4)
        t_a, p_a = white_a[:count_t], white_a[count_t:]
        t_flip_a = inner(t_a, 0, 1)
        t_moved_a = [inner(t_a, s, 0) for s in range(1, nx)]
        p_moved_a = [over_pool(p_a, s) for s in range(1, n_pool)]
        done = fence(step4, step3, [flip4, *moved4, t_flip_a, *t_moved_a, *p_moved_a])

        moved4 = [behind(v, done) for v in moved4]
        fourth = partial([own4] + moved4 + [flip4] + factor_flip(moved4))
        white_b = (jnp.where(top, fourth, second + step3.astype(F32) + step4.astype(F32)) + done).astype(BF)
        later = token(white_b) + done
        t_a, t_flip_a = behind(t_a, later), behind(t_flip_a, later)
        t_moved_a = [behind(v, later) for v in t_moved_a]
        t_b, p_b = white_b[:count_t], white_b[count_t:]
        t_moved_b = [inner(t_b, s, 0) for s in range(1, nx)]
        p_moved_b = [over_pool(p_b, s) for s in range(1, n_pool)]
        t_flip_b = inner(t_b, 0, 1)

        def groups(t, t_moved, t_flip):
            far, far_flip = jnp.concatenate(t_moved, axis=0), jnp.concatenate([inner(v, 0, 1) for v in t_moved], axis=0)
            keep = jnp.where(top, t_flip, t), jnp.where(top, far_flip, far)
            give = jnp.where(top, t, t_flip), jnp.where(top, far, far_flip)
            return keep, give

        keep_a, give_a = groups(t_a, t_moved_a, t_flip_a)
        keep_b, give_b = groups(t_b, t_moved_b, t_flip_b)
        p_far_a, p_far_b = jnp.concatenate(p_moved_a, axis=0), jnp.concatenate(p_moved_b, axis=0)
        p_all_a, p_all_b = jnp.concatenate([p_a, p_far_a], axis=0), jnp.concatenate([p_b, p_far_b], axis=0)

        given_near = along_z(matmul_t(give_a[0], p_a) + matmul_t(give_b[0], p_b), outer)
        give_side = behind(matmul_t(give_a[0], p_far_a) + matmul_t(give_b[0], p_far_b), token(given_near)[:, :1] if n_pool > 2 else token(given_near))
        give_far = matmul_t(give_a[1], p_all_a) + matmul_t(give_b[1], p_all_b)
        if nx == 2:
            given = along_z(jnp.concatenate([give_side, give_far], axis=1), outer)
            given_side, given_far = given[:, :give_side.shape[1]], given[:, give_side.shape[1]:]
        else:
            given_side, given_far = along_z(give_side, outer), along_z(give_far, outer)

        p_squares = square_sum(p_all_a) + square_sum(p_all_b)
        sizes = [p_squares.shape[0], keep_a[0].shape[0], keep_a[1].shape[0]]
        squares = along_z(jnp.concatenate(
            [p_squares] + [square_sum(a) + square_sum(b) for a, b in zip(give_a, give_b)]
        ), outer)
        pool_var = 1.0 + (p_squares + squares[:sizes[0]])

        def log_sums(group, given, offset):
            a, b = keep_a[group], keep_b[group]
            target_var = 1.0 + (square_sum(a) + square_sum(b) + squares[offset:offset + sizes[1 + group]])
            cross = matmul_t(a, p_all_a) + matmul_t(b, p_all_b) + given
            ratio = jnp.square(cross) / (target_var[:, None] * pool_var[None, :])
            return -0.5 * jnp.sum(jnp.log1p(-ratio), axis=0)

        sums = log_sums(0, jnp.concatenate([given_near, given_side], axis=1), sizes[0])
        sums = sums + log_sums(1, given_far, sizes[0] + sizes[1])

        blocks = [sums[s * count:(s + 1) * count] for s in range(n_pool)]
        own = blocks[0] + along_z(blocks[0], outer)
        for s in range(1, n_pool):
            own = own + (over_pool(blocks[s], -s) + over_pool(blocks[s], -s, 0, outer))
        rows = [in_order([own if s == 0 else inner(own, s, 0), inner(own, s, 1)], core) for s in range(nx)]
        scores = in_order(rows, x)
        return jnp.where(z >= nz - 2, scores, along_z(scores, skip))

    return body


def solution(mesh):
    in_specs = (P("pool", "tgt"), P("pool"), P("pool", "tgt"), P("tgt", None))
    out_specs = P("pool")
    body = make_body(mesh.shape["pool"], mesh.shape["tgt"])
    return jax.shard_map(body, mesh=mesh, in_specs=in_specs, out_specs=out_specs, check_vma=False)
```

```python
import jax
import jax.numpy as jnp
from jax import lax
from jax.sharding import PartitionSpec as P

QUARTERS = 4
CORES = 2
BF = jnp.bfloat16
F32 = jnp.float32


def matmul(a, b):
    return lax.dot_general(a, b, (((1,), (0,)), ((), ())), preferred_element_type=F32)


def matmul_t(a, b):
    return lax.dot_general(a, b, (((1,), (1,)), ((), ())), preferred_element_type=F32)


def token(*arrays):
    width = min(v.shape[-1] for v in arrays)
    rows = [lax.slice_in_dim(v.reshape(-1, v.shape[-1])[:1], 0, width, axis=1) for v in arrays]
    return sum(jnp.minimum(jnp.abs(r.astype(F32)), 0.0) for r in rows)


def fence(first, second, others):
    done = lax.optimization_barrier(token(*first))
    done = lax.optimization_barrier(token(*second) + done)
    return token(*others) + done


def behind(value, zeros):
    zeros = zeros if zeros.shape[-1] == 1 else zeros[:, :value.shape[-1]]
    return value + zeros.astype(value.dtype)


def square_sum(a):
    return jnp.sum(jnp.square(a.astype(F32)), axis=1)


def make_body(n_pool, n_tgt):
    nz = QUARTERS
    nx = n_tgt // (nz * CORES)
    outer = (1, 0, 3, 2)
    middle = (0, 2, 1, 3)
    skip = (2, 3, 0, 1)

    def place(z, x, c):
        return (z * nx + x) * CORES + c

    def inner(value, shift, flip):
        pairs = [
            (place(z, x, c), place(z, (x + shift) % nx, c ^ flip))
            for z in range(nz) for x in range(nx) for c in range(CORES)
        ]
        return lax.ppermute(value, "tgt", pairs)

    def along_z(value, to):
        pairs = [
            (place(z, x, c), place(to[z], x, c)) for z in range(nz) for x in range(nx) for c in range(CORES)
        ]
        return lax.ppermute(value, "tgt", pairs)

    def over_pool(value, shift, flip=0, to=None):
        to = to or range(nz)
        pairs = [
            (p * n_tgt + place(z, x, c), ((p + shift) % n_pool) * n_tgt + place(to[z], x, c ^ flip))
            for p in range(n_pool) for z in range(nz) for x in range(nx) for c in range(CORES)
        ]
        return lax.ppermute(value, ("pool", "tgt"), pairs)

    def in_order(pieces, index):
        n = len(pieces)
        if n == 2:
            low = index == 0
            return jnp.concatenate([jnp.where(low, pieces[0], pieces[1]), jnp.where(low, pieces[1], pieces[0])], axis=0)
        stacked = jnp.take(jnp.stack(pieces), (index - jnp.arange(n)) % n, axis=0)
        return stacked.reshape((-1,) + stacked.shape[2:])

    def choose(values, z):
        out = jnp.int32(values[0])
        for k in range(1, nz):
            out = jnp.where(z == k, jnp.int32(values[k]), out)
        return out

    def body(pool_table, pool_index, target_features, posterior_factor):
        me = lax.axis_index("tgt")
        core = me % CORES
        x = (me // CORES) % nx
        z = me // (CORES * nx)
        top = z == nz - 1
        width, hidden = posterior_factor.shape
        quarter = hidden // nz

        local_index = pool_index - lax.axis_index("pool") * pool_table.shape[0]
        pool_rows = pool_table.at[local_index].get(mode="promise_in_bounds")
        count = pool_rows.shape[0] // (nx * CORES)
        count_t = target_features.shape[0] // (nx * CORES)

        rows = jnp.concatenate([
            target_features.reshape(nx, CORES, count_t, width), pool_rows.reshape(nx, CORES, count, width)
        ], axis=2)
        n_rows = count + count_t

        def rows_of(s, f):
            return lax.dynamic_slice(rows, (lax.rem(x + s, nx), core ^ f, 0, 0), (1, 1, n_rows, width))[0, 0]

        def rows_of_both(s):
            return lax.dynamic_index_in_dim(rows, lax.rem(x + s, nx), 0, keepdims=False)

        def factor_own(choice):
            return lax.dynamic_slice_in_dim(posterior_factor, choose(choice, z) * quarter, quarter, 1)

        def factor_x(own):
            return [inner(own, s, 0) for s in range(1, nx)]

        def partial(pieces):
            total = None
            for f, l in zip(features, pieces):
                term = matmul(f, l)
                total = term if total is None else total + term
            return total

        def factor_flip(same):
            return [inner(v, 0, 1) for v in same]

        order = [(s, 0) for s in range(nx)] + [(s, 1) for s in range(nx)]

        pool = lax.axis_index("pool")
        part_rows = width // n_pool
        own1 = lax.optimization_barrier(factor_own([0, 1, 2, 1]))
        mine1 = lax.dynamic_slice_in_dim(own1, pool * part_rows, part_rows, 0)
        parts1 = [inner(mine1, s, 0) for s in range(1, nx)]

        done = token(*parts1)
        features, other = [rows_of(0, 0)], [rows_of(0, 1)]
        for s in range(1, nx):
            both = inner(behind(rows_of_both(s), done), s, 0)
            features.append(lax.dynamic_index_in_dim(both, core, 0, keepdims=False))
            other.append(lax.dynamic_index_in_dim(both, 1 - core, 0, keepdims=False))
        features += [inner(v, 0, 1) for v in other]
        near1 = [in_order([v] + [over_pool(v, r) for r in range(1, n_pool)], pool) for v in parts1]
        first = partial([own1] + near1 + [inner(v, 0, 1) for v in [own1] + near1]).astype(BF)

        start = token(first)
        step1 = along_z(first, outer)
        step2 = along_z(first, middle)
        own2 = behind(factor_own([0, 0, 0, 0]), start)
        own3 = behind(factor_own([1, 1, 1, 2]), start)
        flip2, flip3 = inner(own2, 0, 1), inner(own3, 0, 1)
        moved2, moved3 = factor_x(own2), factor_x(own3)
        done = fence([step2], [step1], [flip2, flip3, *moved2, *moved3])
        moved2, moved3 = [behind(v, done) for v in moved2], [behind(v, done) for v in moved3]
        second = partial([own2] + moved2 + [flip2] + factor_flip(moved2))
        third = partial([own3] + moved3 + [flip3] + factor_flip(moved3))

        start = token(second, third) + done
        step3 = along_z(behind(second, start).astype(BF), outer)
        step4 = along_z((behind(second, start) + step1.astype(F32)).astype(BF), middle)
        white_a = (third + step1.astype(F32) + jnp.where(top, 0.0, step2.astype(F32)) + start).astype(BF)
        own4 = behind(factor_own([3, 3, 3, 3]), start)
        flip4, moved4 = inner(own4, 0, 1), factor_x(own4)
        t_a, p_a = white_a[:count_t], white_a[count_t:]
        t_flip_a = inner(t_a, 0, 1)
        t_moved_a = [inner(t_a, s, 0) for s in range(1, nx)]
        p_moved_a = [over_pool(p_a, s) for s in range(1, n_pool)]
        done = fence([step3, *moved4], [step4], [flip4, t_flip_a, *t_moved_a, *p_moved_a])

        moved4 = [behind(v, done) for v in moved4]
        fourth = partial([own4] + moved4 + [flip4] + factor_flip(moved4))
        t_moved_a = [behind(v, done) for v in t_moved_a]
        white_b = (jnp.where(top, fourth, second + step3.astype(F32) + step4.astype(F32)) + done).astype(BF)
        t_b, p_b = white_b[:count_t], white_b[count_t:]
        t_moved_b = [inner(t_b, s, 0) for s in range(1, nx)]
        p_moved_b = [over_pool(p_b, s) for s in range(1, n_pool)]
        t_flip_b = inner(t_b, 0, 1)

        def groups(t, t_moved, t_flip):
            far, far_flip = jnp.concatenate(t_moved, axis=0), jnp.concatenate([inner(v, 0, 1) for v in t_moved], axis=0)
            keep = jnp.where(top, t_flip, t), jnp.where(top, far_flip, far)
            give = jnp.where(top, t, t_flip), jnp.where(top, far, far_flip)
            return keep, give

        keep_a, give_a = groups(t_a, t_moved_a, t_flip_a)
        keep_b, give_b = groups(t_b, t_moved_b, t_flip_b)
        p_far_a, p_far_b = jnp.concatenate(p_moved_a, axis=0), jnp.concatenate(p_moved_b, axis=0)
        p_all_a, p_all_b = jnp.concatenate([p_a, p_far_a], axis=0), jnp.concatenate([p_b, p_far_b], axis=0)

        given_near = along_z(matmul_t(give_a[0], p_a) + matmul_t(give_b[0], p_b), outer)
        give_side = behind(matmul_t(give_a[0], p_far_a) + matmul_t(give_b[0], p_far_b), token(given_near)[:, :1] if n_pool > 2 else token(given_near))
        give_far = matmul_t(give_a[1], p_all_a) + matmul_t(give_b[1], p_all_b)
        if nx == 2:
            given = along_z(jnp.concatenate([give_side, give_far], axis=1), outer)
            given_side, given_far = given[:, :give_side.shape[1]], given[:, give_side.shape[1]:]
        else:
            given_side, given_far = along_z(give_side, outer), along_z(give_far, outer)

        p_squares = square_sum(p_all_a) + square_sum(p_all_b)
        sizes = [p_squares.shape[0], keep_a[0].shape[0], keep_a[1].shape[0]]
        squares = along_z(jnp.concatenate(
            [p_squares] + [square_sum(a) + square_sum(b) for a, b in zip(give_a, give_b)]
        ), outer)
        pool_var = 1.0 + (p_squares + squares[:sizes[0]])

        def log_sums(group, given, offset):
            a, b = keep_a[group], keep_b[group]
            target_var = 1.0 + (square_sum(a) + square_sum(b) + squares[offset:offset + sizes[1 + group]])
            cross = matmul_t(a, p_all_a) + matmul_t(b, p_all_b) + given
            ratio = jnp.square(cross) / (target_var[:, None] * pool_var[None, :])
            return -0.5 * jnp.sum(jnp.log1p(-ratio), axis=0)

        sums = log_sums(0, jnp.concatenate([given_near, given_side], axis=1), sizes[0])
        sums = sums + log_sums(1, given_far, sizes[0] + sizes[1])

        blocks = [sums[s * count:(s + 1) * count] for s in range(n_pool)]
        own = blocks[0] + along_z(blocks[0], outer)
        for s in range(1, n_pool):
            own = own + (over_pool(blocks[s], -s) + over_pool(blocks[s], -s, 0, outer))
        rows = [in_order([own if s == 0 else inner(own, s, 0), inner(own, s, 1)], core) for s in range(nx)]
        scores = in_order(rows, x)
        return jnp.where(z >= nz - 2, scores, along_z(scores, skip))

    return body


def solution(mesh):
    in_specs = (P("pool", "tgt"), P("pool"), P("pool", "tgt"), P("tgt", None))
    out_specs = P("pool")
    body = make_body(mesh.shape["pool"], mesh.shape["tgt"])
    return jax.shard_map(body, mesh=mesh, in_specs=in_specs, out_specs=out_specs, check_vma=False)
```

```python
import jax
import jax.numpy as jnp
from jax import lax
from jax.sharding import PartitionSpec as P

QUARTERS = 4
CORES = 2
BF = jnp.bfloat16
F32 = jnp.float32


def matmul(a, b):
    return lax.dot_general(a, b, (((1,), (0,)), ((), ())), preferred_element_type=F32)


def matmul_t(a, b):
    return lax.dot_general(a, b, (((1,), (1,)), ((), ())), preferred_element_type=F32)


def token(*arrays):
    width = min(v.shape[-1] for v in arrays)
    rows = [lax.slice_in_dim(v.reshape(-1, v.shape[-1])[:1], 0, width, axis=1) for v in arrays]
    return sum(jnp.minimum(jnp.abs(r.astype(F32)), 0.0) for r in rows)


def fence(first, second, others):
    done = lax.optimization_barrier(token(first))
    done = lax.optimization_barrier(token(second) + done)
    return token(*others) + done


def behind(value, zeros):
    zeros = zeros if zeros.shape[-1] == 1 else zeros[:, :value.shape[-1]]
    return value + zeros.astype(value.dtype)


def square_sum(a):
    return jnp.sum(jnp.square(a.astype(F32)), axis=1)


def make_body(n_pool, n_tgt):
    nz = QUARTERS
    nx = n_tgt // (nz * CORES)
    outer = (1, 0, 3, 2)
    middle = (0, 2, 1, 3)
    skip = (2, 3, 0, 1)

    def place(z, x, c):
        return (z * nx + x) * CORES + c

    def inner(value, shift, flip):
        pairs = [
            (place(z, x, c), place(z, (x + shift) % nx, c ^ flip))
            for z in range(nz) for x in range(nx) for c in range(CORES)
        ]
        return lax.ppermute(value, "tgt", pairs)

    def along_z(value, to):
        pairs = [
            (place(z, x, c), place(to[z], x, c)) for z in range(nz) for x in range(nx) for c in range(CORES)
        ]
        return lax.ppermute(value, "tgt", pairs)

    def over_pool(value, shift, flip=0, to=None):
        to = to or range(nz)
        pairs = [
            (p * n_tgt + place(z, x, c), ((p + shift) % n_pool) * n_tgt + place(to[z], x, c ^ flip))
            for p in range(n_pool) for z in range(nz) for x in range(nx) for c in range(CORES)
        ]
        return lax.ppermute(value, ("pool", "tgt"), pairs)

    def in_order(pieces, index):
        n = len(pieces)
        if n == 2:
            low = index == 0
            return jnp.concatenate([jnp.where(low, pieces[0], pieces[1]), jnp.where(low, pieces[1], pieces[0])], axis=0)
        stacked = jnp.take(jnp.stack(pieces), (index - jnp.arange(n)) % n, axis=0)
        return stacked.reshape((-1,) + stacked.shape[2:])

    def choose(values, z):
        out = jnp.int32(values[0])
        for k in range(1, nz):
            out = jnp.where(z == k, jnp.int32(values[k]), out)
        return out

    def body(pool_table, pool_index, target_features, posterior_factor):
        me = lax.axis_index("tgt")
        core = me % CORES
        x = (me // CORES) % nx
        z = me // (CORES * nx)
        top = z == nz - 1
        width, hidden = posterior_factor.shape
        quarter = hidden // nz

        local_index = pool_index - lax.axis_index("pool") * pool_table.shape[0]
        pool_rows = pool_table.at[local_index].get(mode="promise_in_bounds")
        count = pool_rows.shape[0] // (nx * CORES)
        count_t = target_features.shape[0] // (nx * CORES)

        rows = jnp.concatenate([
            target_features.reshape(nx, CORES, count_t, width), pool_rows.reshape(nx, CORES, count, width)
        ], axis=2)
        n_rows = count + count_t

        def rows_of(s, f):
            return lax.dynamic_slice(rows, (lax.rem(x + s, nx), core ^ f, 0, 0), (1, 1, n_rows, width))[0, 0]

        def factor_own(choice):
            return lax.dynamic_slice_in_dim(posterior_factor, choose(choice, z) * quarter, quarter, 1)

        def factor_x(own):
            return [inner(own, s, 0) for s in range(1, nx)]

        def partial(pieces):
            total = None
            for f, l in zip(features, pieces):
                term = matmul(f, l)
                total = term if total is None else total + term
            return total

        def factor_flip(same):
            return [inner(v, 0, 1) for v in same]

        order = [(s, 0) for s in range(nx)] + [(s, 1) for s in range(nx)]

        own1 = factor_own([0, 1, 2, 1])
        same1 = [own1] + factor_x(own1)

        done = token(*same1[1:])
        features = [inner(behind(rows_of(s, f), done), s, f) if s or f else rows_of(0, 0) for s, f in order]
        first = partial(same1 + factor_flip(same1)).astype(BF)

        start = token(first)
        step1 = along_z(first, outer)
        step2 = along_z(first, middle)
        own2 = behind(factor_own([0, 0, 0, 0]), start)
        own3 = behind(factor_own([1, 1, 1, 2]), start)
        flip2, flip3 = inner(own2, 0, 1), inner(own3, 0, 1)
        moved2, moved3 = factor_x(own2), factor_x(own3)
        done = fence(step2, step1, [flip2, flip3, *moved2, *moved3])
        moved2, moved3 = [behind(v, done) for v in moved2], [behind(v, done) for v in moved3]
        second = partial([own2] + moved2 + [flip2] + factor_flip(moved2))
        third = partial([own3] + moved3 + [flip3] + factor_flip(moved3))

        start = token(second, third) + done
        step3 = along_z(behind(second, start).astype(BF), outer)
        step4 = along_z((behind(second, start) + step1.astype(F32)).astype(BF), middle)
        white_a = (third + step1.astype(F32) + jnp.where(top, 0.0, step2.astype(F32)) + start).astype(BF)
        own4 = behind(factor_own([3, 3, 3, 3]), start)
        flip4, moved4 = inner(own4, 0, 1), factor_x(own4)
        t_a, p_a = white_a[:count_t], white_a[count_t:]
        t_flip_a = inner(t_a, 0, 1)
        t_moved_a = [inner(t_a, s, 0) for s in range(1, nx)]
        p_moved_a = [over_pool(p_a, s) for s in range(1, n_pool)]
        done = fence(step3, step4, [flip4, *moved4, t_flip_a, *t_moved_a, *p_moved_a])

        moved4 = [behind(v, done) for v in moved4]
        fourth = partial([own4] + moved4 + [flip4] + factor_flip(moved4))
        t_moved_a = [behind(v, done) for v in t_moved_a]
        white_b = (jnp.where(top, fourth, second + step3.astype(F32) + step4.astype(F32)) + done).astype(BF)
        t_b, p_b = white_b[:count_t], white_b[count_t:]
        t_moved_b = [inner(t_b, s, 0) for s in range(1, nx)]
        p_moved_b = [over_pool(p_b, s) for s in range(1, n_pool)]
        t_flip_b = inner(t_b, 0, 1)

        def groups(t, t_moved, t_flip):
            far, far_flip = jnp.concatenate(t_moved, axis=0), jnp.concatenate([inner(v, 0, 1) for v in t_moved], axis=0)
            keep = jnp.where(top, t_flip, t), jnp.where(top, far_flip, far)
            give = jnp.where(top, t, t_flip), jnp.where(top, far, far_flip)
            return keep, give

        keep_a, give_a = groups(t_a, t_moved_a, t_flip_a)
        keep_b, give_b = groups(t_b, t_moved_b, t_flip_b)
        p_far_a, p_far_b = jnp.concatenate(p_moved_a, axis=0), jnp.concatenate(p_moved_b, axis=0)
        p_all_a, p_all_b = jnp.concatenate([p_a, p_far_a], axis=0), jnp.concatenate([p_b, p_far_b], axis=0)

        given_near = along_z(matmul_t(give_a[0], p_a) + matmul_t(give_b[0], p_b), outer)
        give_side = behind(matmul_t(give_a[0], p_far_a) + matmul_t(give_b[0], p_far_b), token(given_near)[:, :1] if n_pool > 2 else token(given_near))
        give_far = matmul_t(give_a[1], p_all_a) + matmul_t(give_b[1], p_all_b)
        if nx == 2:
            given = along_z(jnp.concatenate([give_side, give_far], axis=1), outer)
            given_side, given_far = given[:, :give_side.shape[1]], given[:, give_side.shape[1]:]
        else:
            given_side, given_far = along_z(give_side, outer), along_z(give_far, outer)

        p_squares = square_sum(p_all_a) + square_sum(p_all_b)
        sizes = [p_squares.shape[0], keep_a[0].shape[0], keep_a[1].shape[0]]
        squares = along_z(jnp.concatenate(
            [p_squares] + [square_sum(a) + square_sum(b) for a, b in zip(give_a, give_b)]
        ), outer)
        pool_var = 1.0 + (p_squares + squares[:sizes[0]])

        def log_sums(group, given, offset):
            a, b = keep_a[group], keep_b[group]
            target_var = 1.0 + (square_sum(a) + square_sum(b) + squares[offset:offset + sizes[1 + group]])
            cross = matmul_t(a, p_all_a) + matmul_t(b, p_all_b) + given
            ratio = jnp.square(cross) / (target_var[:, None] * pool_var[None, :])
            return -0.5 * jnp.sum(jnp.log1p(-ratio), axis=0)

        sums = log_sums(0, jnp.concatenate([given_near, given_side], axis=1), sizes[0])
        sums = sums + log_sums(1, given_far, sizes[0] + sizes[1])

        blocks = [sums[s * count:(s + 1) * count] for s in range(n_pool)]
        own = blocks[0] + along_z(blocks[0], outer)
        for s in range(1, n_pool):
            own = own + (over_pool(blocks[s], -s) + over_pool(blocks[s], -s, 0, outer))
        rows = [in_order([own if s == 0 else inner(own, s, 0), inner(own, s, 1)], core) for s in range(nx)]
        scores = in_order(rows, x)
        return jnp.where(z >= nz - 2, scores, along_z(scores, skip))

    return body


def solution(mesh):
    in_specs = (P("pool", "tgt"), P("pool"), P("pool", "tgt"), P("tgt", None))
    out_specs = P("pool")
    body = make_body(mesh.shape["pool"], mesh.shape["tgt"])
    return jax.shard_map(body, mesh=mesh, in_specs=in_specs, out_specs=out_specs, check_vma=False)
```

```python
import jax
import jax.numpy as jnp
from jax import lax
from jax.sharding import PartitionSpec as P

QUARTERS = 4
CORES = 2
BF = jnp.bfloat16
F32 = jnp.float32


def matmul(a, b):
    return lax.dot_general(a, b, (((1,), (0,)), ((), ())), preferred_element_type=F32)


def matmul_t(a, b):
    return lax.dot_general(a, b, (((1,), (1,)), ((), ())), preferred_element_type=F32)


def token(*arrays):
    width = min(v.shape[-1] for v in arrays)
    rows = [lax.slice_in_dim(v.reshape(-1, v.shape[-1])[:1], 0, width, axis=1) for v in arrays]
    return sum(jnp.minimum(jnp.abs(r.astype(F32)), 0.0) for r in rows)


def fence(first, second, others):
    done = lax.optimization_barrier(token(first))
    done = lax.optimization_barrier(token(second) + done)
    return token(*others) + done


def behind(value, zeros):
    zeros = zeros if zeros.shape[-1] == 1 else zeros[:, :value.shape[-1]]
    return value + zeros.astype(value.dtype)


def square_sum(a):
    return jnp.sum(jnp.square(a.astype(F32)), axis=1)


def make_body(n_pool, n_tgt):
    nz = QUARTERS
    nx = n_tgt // (nz * CORES)
    outer = (1, 0, 3, 2)
    owners = (0, 1, 3, 2)
    middle = (0, 2, 1, 3)
    skip = (2, 3, 0, 1)

    def place(z, x, c):
        return (z * nx + x) * CORES + c

    def inner(value, shift, flip):
        pairs = [
            (place(z, x, c), place(z, (x + shift) % nx, c ^ flip))
            for z in range(nz) for x in range(nx) for c in range(CORES)
        ]
        return lax.ppermute(value, "tgt", pairs)

    def along_z(value, to):
        pairs = [
            (place(z, x, c), place(to[z], x, c)) for z in range(nz) for x in range(nx) for c in range(CORES)
        ]
        return lax.ppermute(value, "tgt", pairs)

    def over_pool(value, shift, flip=0, to=None):
        to = to or range(nz)
        pairs = [
            (p * n_tgt + place(z, x, c), ((p + shift) % n_pool) * n_tgt + place(to[z], x, c ^ flip))
            for p in range(n_pool) for z in range(nz) for x in range(nx) for c in range(CORES)
        ]
        return lax.ppermute(value, ("pool", "tgt"), pairs)

    def in_order(pieces, index):
        n = len(pieces)
        if n == 2:
            low = index == 0
            return jnp.concatenate([jnp.where(low, pieces[0], pieces[1]), jnp.where(low, pieces[1], pieces[0])], axis=0)
        stacked = jnp.take(jnp.stack(pieces), (index - jnp.arange(n)) % n, axis=0)
        return stacked.reshape((-1,) + stacked.shape[2:])

    def choose(values, z):
        out = jnp.int32(values[0])
        for k in range(1, nz):
            out = jnp.where(z == k, jnp.int32(values[k]), out)
        return out

    def body(pool_table, pool_index, target_features, posterior_factor):
        me = lax.axis_index("tgt")
        core = me % CORES
        x = (me // CORES) % nx
        z = me // (CORES * nx)
        top = z == nz - 1
        width, hidden = posterior_factor.shape
        quarter = hidden // nz

        local_index = pool_index - lax.axis_index("pool") * pool_table.shape[0]
        pool_rows = pool_table.at[local_index].get(mode="promise_in_bounds")
        count = pool_rows.shape[0] // (nx * CORES)
        count_t = target_features.shape[0] // (nx * CORES)

        rows = jnp.concatenate([
            target_features.reshape(nx, CORES, count_t, width), pool_rows.reshape(nx, CORES, count, width)
        ], axis=2)
        n_rows = count + count_t

        def rows_of(s, f):
            return lax.dynamic_slice(rows, (lax.rem(x + s, nx), core ^ f, 0, 0), (1, 1, n_rows, width))[0, 0]

        def factor_own(choice):
            return lax.dynamic_slice_in_dim(posterior_factor, choose(choice, z) * quarter, quarter, 1)

        def factor_x(own):
            return [inner(own, s, 0) for s in range(1, nx)]

        def partial(pieces):
            total = None
            for f, l in zip(features, pieces):
                term = matmul(f, l)
                total = term if total is None else total + term
            return total

        def factor_flip(same):
            return [inner(v, 0, 1) for v in same]

        order = [(s, 0) for s in range(nx)] + [(s, 1) for s in range(nx)]

        own1 = factor_own([0, 1, 2, 1])
        same1 = [own1] + factor_x(own1)

        done = token(*same1[1:])
        features = [inner(behind(rows_of(s, f), done), s, f) if s or f else rows_of(0, 0) for s, f in order]
        first = partial(same1 + factor_flip(same1)).astype(BF)

        start = token(first)
        step1 = along_z(first, outer)
        step2 = along_z(first, middle)
        own2 = behind(factor_own([0, 0, 0, 0]), start)
        own3 = behind(factor_own([1, 1, 1, 2]), start)
        flip2, flip3 = inner(own2, 0, 1), inner(own3, 0, 1)
        moved2, moved3 = factor_x(own2), factor_x(own3)
        done = fence(step2, step1, [flip2, flip3, *moved2, *moved3])
        moved2, moved3 = [behind(v, done) for v in moved2], [behind(v, done) for v in moved3]
        second = partial([own2] + moved2 + [flip2] + factor_flip(moved2))
        third = partial([own3] + moved3 + [flip3] + factor_flip(moved3))

        start = token(second, third) + done
        step3 = along_z(behind(second, start).astype(BF), owners)
        step4 = along_z((behind(second, start) + step1.astype(F32)).astype(BF), middle)
        white_a = (third + step1.astype(F32) + jnp.where(top, 0.0, step2.astype(F32)) + start).astype(BF)
        own4 = behind(factor_own([3, 3, 3, 3]), start)
        flip4, moved4 = inner(own4, 0, 1), factor_x(own4)
        t_a, p_a = white_a[:count_t], white_a[count_t:]
        t_flip_a = inner(t_a, 0, 1)
        t_moved_a = [inner(t_a, s, 0) for s in range(1, nx)]
        p_moved_a = [over_pool(p_a, s) for s in range(1, n_pool)]
        done = fence(step3, step4, [flip4, *moved4, t_flip_a, *t_moved_a, *p_moved_a])

        moved4 = [behind(v, done) for v in moved4]
        fourth = partial([own4] + moved4 + [flip4] + factor_flip(moved4))
        t_moved_a = [behind(v, done) for v in t_moved_a]
        white_b = (jnp.where(top, fourth, second + step3.astype(F32) + step4.astype(F32)) + done).astype(BF)
        t_b, p_b = white_b[:count_t], white_b[count_t:]
        t_moved_b = [inner(t_b, s, 0) for s in range(1, nx)]
        p_moved_b = [over_pool(p_b, s) for s in range(1, n_pool)]
        t_flip_b = inner(t_b, 0, 1)

        def groups(t, t_moved, t_flip):
            far, far_flip = jnp.concatenate(t_moved, axis=0), jnp.concatenate([inner(v, 0, 1) for v in t_moved], axis=0)
            keep = jnp.where(top, t_flip, t), jnp.where(top, far_flip, far)
            give = jnp.where(top, t, t_flip), jnp.where(top, far, far_flip)
            return keep, give

        keep_a, give_a = groups(t_a, t_moved_a, t_flip_a)
        keep_b, give_b = groups(t_b, t_moved_b, t_flip_b)
        p_far_a, p_far_b = jnp.concatenate(p_moved_a, axis=0), jnp.concatenate(p_moved_b, axis=0)
        p_all_a, p_all_b = jnp.concatenate([p_a, p_far_a], axis=0), jnp.concatenate([p_b, p_far_b], axis=0)

        given_near = along_z(matmul_t(give_a[0], p_a) + matmul_t(give_b[0], p_b), owners)
        give_side = behind(matmul_t(give_a[0], p_far_a) + matmul_t(give_b[0], p_far_b), token(given_near)[:, :1] if n_pool > 2 else token(given_near))
        give_far = matmul_t(give_a[1], p_all_a) + matmul_t(give_b[1], p_all_b)
        if nx == 2:
            given = along_z(jnp.concatenate([give_side, give_far], axis=1), owners)
            given_side, given_far = given[:, :give_side.shape[1]], given[:, give_side.shape[1]:]
        else:
            given_side, given_far = along_z(give_side, owners), along_z(give_far, owners)

        p_squares = square_sum(p_all_a) + square_sum(p_all_b)
        sizes = [p_squares.shape[0], keep_a[0].shape[0], keep_a[1].shape[0]]
        squares = along_z(jnp.concatenate(
            [p_squares] + [square_sum(a) + square_sum(b) for a, b in zip(give_a, give_b)]
        ), owners)
        pool_var = 1.0 + (p_squares + squares[:sizes[0]])

        def log_sums(group, given, offset):
            a, b = keep_a[group], keep_b[group]
            target_var = 1.0 + (square_sum(a) + square_sum(b) + squares[offset:offset + sizes[1 + group]])
            cross = matmul_t(a, p_all_a) + matmul_t(b, p_all_b) + given
            ratio = jnp.square(cross) / (target_var[:, None] * pool_var[None, :])
            return -0.5 * jnp.sum(jnp.log1p(-ratio), axis=0)

        sums = log_sums(0, jnp.concatenate([given_near, given_side], axis=1), sizes[0])
        sums = sums + log_sums(1, given_far, sizes[0] + sizes[1])

        blocks = [sums[s * count:(s + 1) * count] for s in range(n_pool)]
        own = blocks[0] + along_z(blocks[0], owners)
        for s in range(1, n_pool):
            own = own + (over_pool(blocks[s], -s) + over_pool(blocks[s], -s, 0, owners))
        rows = [in_order([own if s == 0 else inner(own, s, 0), inner(own, s, 1)], core) for s in range(nx)]
        scores = in_order(rows, x)
        return jnp.where(z >= nz - 2, scores, along_z(scores, skip))

    return body


def solution(mesh):
    in_specs = (P("pool", "tgt"), P("pool"), P("pool", "tgt"), P("tgt", None))
    out_specs = P("pool")
    body = make_body(mesh.shape["pool"], mesh.shape["tgt"])
    return jax.shard_map(body, mesh=mesh, in_specs=in_specs, out_specs=out_specs, check_vma=False)
```

```python
import jax
import jax.numpy as jnp
from jax import lax
from jax.sharding import PartitionSpec as P

QUARTERS = 4
CORES = 2
BF = jnp.bfloat16
F32 = jnp.float32


def matmul(a, b):
    return lax.dot_general(a, b, (((1,), (0,)), ((), ())), preferred_element_type=F32)


def matmul_t(a, b):
    return lax.dot_general(a, b, (((1,), (1,)), ((), ())), preferred_element_type=F32)


def token(*arrays):
    width = min(v.shape[-1] for v in arrays)
    rows = [lax.slice_in_dim(v.reshape(-1, v.shape[-1])[:1], 0, width, axis=1) for v in arrays]
    return sum(jnp.minimum(jnp.abs(r.astype(F32)), 0.0) for r in rows)


def fence(first, second, others):
    done = lax.optimization_barrier(token(first))
    done = lax.optimization_barrier(token(second) + done)
    return token(*others) + done


def behind(value, zeros):
    zeros = zeros if zeros.shape[-1] == 1 else zeros[:, :value.shape[-1]]
    return value + zeros.astype(value.dtype)


def square_sum(a):
    return jnp.sum(jnp.square(a.astype(F32)), axis=1)


def make_body(n_pool, n_tgt):
    nz = QUARTERS
    nx = n_tgt // (nz * CORES)
    outer = (1, 0, 3, 2)
    owners = (0, 1, 3, 2)
    middle = (0, 2, 1, 3)
    skip = (2, 3, 0, 1)

    def place(z, x, c):
        return (z * nx + x) * CORES + c

    def inner(value, shift, flip):
        pairs = [
            (place(z, x, c), place(z, (x + shift) % nx, c ^ flip))
            for z in range(nz) for x in range(nx) for c in range(CORES)
        ]
        return lax.ppermute(value, "tgt", pairs)

    def along_z(value, to):
        pairs = [
            (place(z, x, c), place(to[z], x, c ^ (to[z] == z)))
            for z in range(nz) for x in range(nx) for c in range(CORES)
        ]
        return lax.ppermute(value, "tgt", pairs)

    def over_pool(value, shift, flip=0, to=None):
        to = to or range(nz)
        pairs = [
            (p * n_tgt + place(z, x, c), ((p + shift) % n_pool) * n_tgt + place(to[z], x, c ^ flip))
            for p in range(n_pool) for z in range(nz) for x in range(nx) for c in range(CORES)
        ]
        return lax.ppermute(value, ("pool", "tgt"), pairs)

    def in_order(pieces, index):
        n = len(pieces)
        if n == 2:
            low = index == 0
            return jnp.concatenate([jnp.where(low, pieces[0], pieces[1]), jnp.where(low, pieces[1], pieces[0])], axis=0)
        stacked = jnp.take(jnp.stack(pieces), (index - jnp.arange(n)) % n, axis=0)
        return stacked.reshape((-1,) + stacked.shape[2:])

    def choose(values, z):
        out = jnp.int32(values[0])
        for k in range(1, nz):
            out = jnp.where(z == k, jnp.int32(values[k]), out)
        return out

    def body(pool_table, pool_index, target_features, posterior_factor):
        me = lax.axis_index("tgt")
        core = me % CORES
        x = (me // CORES) % nx
        z = me // (CORES * nx)
        top = z == nz - 1
        width, hidden = posterior_factor.shape
        quarter = hidden // nz

        local_index = pool_index - lax.axis_index("pool") * pool_table.shape[0]
        pool_rows = pool_table.at[local_index].get(mode="promise_in_bounds")
        count = pool_rows.shape[0] // (nx * CORES)
        count_t = target_features.shape[0] // (nx * CORES)

        rows = jnp.concatenate([
            target_features.reshape(nx, CORES, count_t, width), pool_rows.reshape(nx, CORES, count, width)
        ], axis=2)
        n_rows = count + count_t

        def rows_of(s, f):
            return lax.dynamic_slice(rows, (lax.rem(x + s, nx), core ^ f, 0, 0), (1, 1, n_rows, width))[0, 0]

        def factor_own(choice):
            return lax.dynamic_slice_in_dim(posterior_factor, choose(choice, z) * quarter, quarter, 1)

        def factor_x(own):
            return [inner(own, s, 0) for s in range(1, nx)]

        def partial(pieces):
            total = None
            for f, l in zip(features, pieces):
                term = matmul(f, l)
                total = term if total is None else total + term
            return total

        def factor_flip(same):
            return [inner(v, 0, 1) for v in same]

        order = [(s, 0) for s in range(nx)] + [(s, 1) for s in range(nx)]

        own1 = factor_own([0, 1, 2, 1])
        same1 = [own1] + factor_x(own1)

        done = token(*same1[1:])
        features = [inner(behind(rows_of(s, f), done), s, f) if s or f else rows_of(0, 0) for s, f in order]
        first = partial(same1 + factor_flip(same1)).astype(BF)

        start = token(first)
        step1 = along_z(first, outer)
        step2 = along_z(first, middle)
        own2 = behind(factor_own([0, 0, 0, 0]), start)
        own3 = behind(factor_own([1, 1, 1, 2]), start)
        flip2, flip3 = inner(own2, 0, 1), inner(own3, 0, 1)
        moved2, moved3 = factor_x(own2), factor_x(own3)
        done = fence(step2, step1, [flip2, flip3, *moved2, *moved3])
        moved2, moved3 = [behind(v, done) for v in moved2], [behind(v, done) for v in moved3]
        second = partial([own2] + moved2 + [flip2] + factor_flip(moved2))
        third = partial([own3] + moved3 + [flip3] + factor_flip(moved3))

        start = token(second, third) + done
        step3 = along_z(behind(second, start).astype(BF), owners)
        step4 = along_z((behind(second, start) + step1.astype(F32)).astype(BF), middle)
        white_a = (third + step1.astype(F32) + jnp.where(top, 0.0, step2.astype(F32)) + start).astype(BF)
        own4 = behind(factor_own([3, 3, 3, 3]), start)
        flip4, moved4 = inner(own4, 0, 1), factor_x(own4)
        t_a, p_a = white_a[:count_t], white_a[count_t:]
        t_flip_a = inner(t_a, 0, 1)
        t_moved_a = [inner(t_a, s, 0) for s in range(1, nx)]
        p_moved_a = [over_pool(p_a, s) for s in range(1, n_pool)]
        done = fence(step3, step4, [flip4, *moved4, t_flip_a, *t_moved_a, *p_moved_a])

        moved4 = [behind(v, done) for v in moved4]
        fourth = partial([own4] + moved4 + [flip4] + factor_flip(moved4))
        t_moved_a = [behind(v, done) for v in t_moved_a]
        white_b = (jnp.where(top, fourth, second + step3.astype(F32) + step4.astype(F32)) + done).astype(BF)
        t_b, p_b = white_b[:count_t], white_b[count_t:]
        t_moved_b = [inner(t_b, s, 0) for s in range(1, nx)]
        p_moved_b = [over_pool(p_b, s) for s in range(1, n_pool)]
        t_flip_b = inner(t_b, 0, 1)

        def groups(t, t_moved, t_flip):
            far, far_flip = jnp.concatenate(t_moved, axis=0), jnp.concatenate([inner(v, 0, 1) for v in t_moved], axis=0)
            keep = jnp.where(top, t_flip, t), jnp.where(top, far_flip, far)
            give = jnp.where(top, t, t_flip), jnp.where(top, far, far_flip)
            return keep, give

        keep_a, give_a = groups(t_a, t_moved_a, t_flip_a)
        keep_b, give_b = groups(t_b, t_moved_b, t_flip_b)
        p_far_a, p_far_b = jnp.concatenate(p_moved_a, axis=0), jnp.concatenate(p_moved_b, axis=0)
        p_all_a, p_all_b = jnp.concatenate([p_a, p_far_a], axis=0), jnp.concatenate([p_b, p_far_b], axis=0)

        given_near = along_z(matmul_t(give_a[0], p_a) + matmul_t(give_b[0], p_b), owners)
        give_side = behind(matmul_t(give_a[0], p_far_a) + matmul_t(give_b[0], p_far_b), token(given_near)[:, :1] if n_pool > 2 else token(given_near))
        give_far = matmul_t(give_a[1], p_all_a) + matmul_t(give_b[1], p_all_b)
        if nx == 2:
            given = along_z(jnp.concatenate([give_side, give_far], axis=1), owners)
            given_side, given_far = given[:, :give_side.shape[1]], given[:, give_side.shape[1]:]
        else:
            given_side, given_far = along_z(give_side, owners), along_z(give_far, owners)

        p_squares = square_sum(p_all_a) + square_sum(p_all_b)
        sizes = [p_squares.shape[0], keep_a[0].shape[0], keep_a[1].shape[0]]
        squares = along_z(jnp.concatenate(
            [p_squares] + [square_sum(a) + square_sum(b) for a, b in zip(give_a, give_b)]
        ), owners)
        pool_var = 1.0 + (p_squares + squares[:sizes[0]])

        def log_sums(group, given, offset):
            a, b = keep_a[group], keep_b[group]
            target_var = 1.0 + (square_sum(a) + square_sum(b) + squares[offset:offset + sizes[1 + group]])
            cross = matmul_t(a, p_all_a) + matmul_t(b, p_all_b) + given
            ratio = jnp.square(cross) / (target_var[:, None] * pool_var[None, :])
            return -0.5 * jnp.sum(jnp.log1p(-ratio), axis=0)

        sums = log_sums(0, jnp.concatenate([given_near, given_side], axis=1), sizes[0])
        sums = sums + log_sums(1, given_far, sizes[0] + sizes[1])

        blocks = [sums[s * count:(s + 1) * count] for s in range(n_pool)]
        own = blocks[0] + along_z(blocks[0], owners)
        for s in range(1, n_pool):
            own = own + (over_pool(blocks[s], -s) + over_pool(blocks[s], -s, 0, owners))
        rows = [in_order([own if s == 0 else inner(own, s, 0), inner(own, s, 1)], core) for s in range(nx)]
        scores = in_order(rows, x)
        return jnp.where(z >= nz - 2, scores, along_z(scores, skip))

    return body


def solution(mesh):
    in_specs = (P("pool", "tgt"), P("pool"), P("pool", "tgt"), P("tgt", None))
    out_specs = P("pool")
    body = make_body(mesh.shape["pool"], mesh.shape["tgt"])
    return jax.shard_map(body, mesh=mesh, in_specs=in_specs, out_specs=out_specs, check_vma=False)
```

```python
import jax
import jax.numpy as jnp
from jax import lax
from jax.sharding import PartitionSpec as P

QUARTERS = 4
CORES = 2
BF = jnp.bfloat16
F32 = jnp.float32


def matmul(a, b):
    return lax.dot_general(a, b, (((1,), (0,)), ((), ())), preferred_element_type=F32)


def matmul_t(a, b):
    return lax.dot_general(a, b, (((1,), (1,)), ((), ())), preferred_element_type=F32)


def token(*arrays):
    width = min(v.shape[-1] for v in arrays)
    rows = [lax.slice_in_dim(v.reshape(-1, v.shape[-1])[:1], 0, width, axis=1) for v in arrays]
    return sum(jnp.minimum(jnp.abs(r.astype(F32)), 0.0) for r in rows)


def fence(first, second, others):
    done = lax.optimization_barrier(token(*first))
    done = lax.optimization_barrier(token(*second) + done)
    return token(*others) + done


def behind(value, zeros):
    zeros = zeros if zeros.shape[-1] == 1 else zeros[:, :value.shape[-1]]
    return value + zeros.astype(value.dtype)


def square_sum(a):
    return jnp.sum(jnp.square(a.astype(F32)), axis=1)


def make_body(n_pool, n_tgt):
    nz = QUARTERS
    nx = n_tgt // (nz * CORES)
    outer = (1, 0, 3, 2)
    owners = (0, 1, 3, 2)
    middle = (0, 2, 1, 3)
    skip = (2, 3, 0, 1)

    def place(z, x, c):
        return (z * nx + x) * CORES + c

    def inner(value, shift, flip):
        pairs = [
            (place(z, x, c), place(z, (x + shift) % nx, c ^ flip))
            for z in range(nz) for x in range(nx) for c in range(CORES)
        ]
        return lax.ppermute(value, "tgt", pairs)

    def along_z(value, to):
        pairs = [
            (place(z, x, c), place(to[z], x, c ^ (to[z] == z)))
            for z in range(nz) for x in range(nx) for c in range(CORES)
        ]
        return lax.ppermute(value, "tgt", pairs)

    def over_pool(value, shift, flip=0, to=None):
        to = to or range(nz)
        pairs = [
            (p * n_tgt + place(z, x, c), ((p + shift) % n_pool) * n_tgt + place(to[z], x, c ^ flip))
            for p in range(n_pool) for z in range(nz) for x in range(nx) for c in range(CORES)
        ]
        return lax.ppermute(value, ("pool", "tgt"), pairs)

    def in_order(pieces, index):
        n = len(pieces)
        if n == 2:
            low = index == 0
            return jnp.concatenate([jnp.where(low, pieces[0], pieces[1]), jnp.where(low, pieces[1], pieces[0])], axis=0)
        stacked = jnp.take(jnp.stack(pieces), (index - jnp.arange(n)) % n, axis=0)
        return stacked.reshape((-1,) + stacked.shape[2:])

    def choose(values, z):
        out = jnp.int32(values[0])
        for k in range(1, nz):
            out = jnp.where(z == k, jnp.int32(values[k]), out)
        return out

    def body(pool_table, pool_index, target_features, posterior_factor):
        me = lax.axis_index("tgt")
        core = me % CORES
        x = (me // CORES) % nx
        z = me // (CORES * nx)
        top = z == nz - 1
        width, hidden = posterior_factor.shape
        quarter = hidden // nz

        local_index = pool_index - lax.axis_index("pool") * pool_table.shape[0]
        pool_rows = pool_table.at[local_index].get(mode="promise_in_bounds")
        count = pool_rows.shape[0] // (nx * CORES)
        count_t = target_features.shape[0] // (nx * CORES)

        rows = jnp.concatenate([
            target_features.reshape(nx, CORES, count_t, width), pool_rows.reshape(nx, CORES, count, width)
        ], axis=2)
        n_rows = count + count_t

        def rows_of(s, f):
            return lax.dynamic_slice(rows, (lax.rem(x + s, nx), core ^ f, 0, 0), (1, 1, n_rows, width))[0, 0]

        def factor_own(choice):
            return lax.dynamic_slice_in_dim(posterior_factor, choose(choice, z) * quarter, quarter, 1)

        def factor_x(own):
            return [inner(own, s, 0) for s in range(1, nx)]

        def partial(pieces):
            total = None
            for f, l in zip(features, pieces):
                term = matmul(f, l)
                total = term if total is None else total + term
            return total

        def factor_flip(same):
            return [inner(v, 0, 1) for v in same]

        order = [(s, 0) for s in range(nx)] + [(s, 1) for s in range(nx)]

        own1 = factor_own([0, 1, 2, 1])
        same1 = [own1] + factor_x(own1)

        done = token(*same1[1:])
        features = [inner(behind(rows_of(s, f), done), s, f) if s or f else rows_of(0, 0) for s, f in order]
        first = partial(same1 + factor_flip(same1)).astype(BF)

        start = token(first)
        step1 = along_z(first, outer)
        step2 = along_z(first, middle)
        own2 = behind(factor_own([0, 0, 0, 0]), start)
        own3 = behind(factor_own([1, 1, 1, 2]), start)
        own4 = behind(factor_own([3, 3, 3, 3]), start)
        flip2, flip3, flip4 = inner(own2, 0, 1), inner(own3, 0, 1), inner(own4, 0, 1)
        moved2, moved3 = factor_x(own2), factor_x(own3)
        done = fence([step2, step1], [*moved2, *moved3], [flip2, flip3, flip4])
        moved2, moved3 = [behind(v, done) for v in moved2], [behind(v, done) for v in moved3]
        second = partial([own2] + moved2 + [flip2] + factor_flip(moved2))
        third = partial([own3] + moved3 + [flip3] + factor_flip(moved3))

        start = token(second, third) + done
        step3 = along_z(behind(second, start).astype(BF), owners)
        step4 = along_z((behind(second, start) + step1.astype(F32)).astype(BF), middle)
        white_a = (third + step1.astype(F32) + jnp.where(top, 0.0, step2.astype(F32)) + start).astype(BF)
        moved4 = factor_x(behind(own4, start))
        t_a, p_a = white_a[:count_t], white_a[count_t:]
        t_moved_a = [inner(t_a, s, 0) for s in range(1, nx)]
        p_moved_a = [over_pool(p_a, s) for s in range(1, n_pool)]
        done = fence([step3, step4], [*moved4, *t_moved_a], p_moved_a)

        moved4 = [behind(v, done) for v in moved4]
        fourth = partial([own4] + moved4 + [flip4] + factor_flip(moved4))
        t_moved_a = [behind(v, done) for v in t_moved_a]
        t_flip_a = inner(behind(t_a, done), 0, 1)
        white_b = (jnp.where(top, fourth, second + step3.astype(F32) + step4.astype(F32)) + done).astype(BF)
        t_b, p_b = white_b[:count_t], white_b[count_t:]
        t_moved_b = [inner(t_b, s, 0) for s in range(1, nx)]
        p_moved_b = [over_pool(p_b, s) for s in range(1, n_pool)]
        t_flip_b = inner(t_b, 0, 1)

        def groups(t, t_moved, t_flip):
            far, far_flip = jnp.concatenate(t_moved, axis=0), jnp.concatenate([inner(v, 0, 1) for v in t_moved], axis=0)
            keep = jnp.where(top, t_flip, t), jnp.where(top, far_flip, far)
            give = jnp.where(top, t, t_flip), jnp.where(top, far, far_flip)
            return keep, give

        keep_a, give_a = groups(t_a, t_moved_a, t_flip_a)
        keep_b, give_b = groups(t_b, t_moved_b, t_flip_b)
        p_far_a, p_far_b = jnp.concatenate(p_moved_a, axis=0), jnp.concatenate(p_moved_b, axis=0)
        p_all_a, p_all_b = jnp.concatenate([p_a, p_far_a], axis=0), jnp.concatenate([p_b, p_far_b], axis=0)

        given_near = along_z(matmul_t(give_a[0], p_a) + matmul_t(give_b[0], p_b), owners)
        give_side = behind(matmul_t(give_a[0], p_far_a) + matmul_t(give_b[0], p_far_b), token(given_near)[:, :1] if n_pool > 2 else token(given_near))
        give_far = matmul_t(give_a[1], p_all_a) + matmul_t(give_b[1], p_all_b)
        if nx == 2:
            given = along_z(jnp.concatenate([give_side, give_far], axis=1), owners)
            given_side, given_far = given[:, :give_side.shape[1]], given[:, give_side.shape[1]:]
        else:
            given_side, given_far = along_z(give_side, owners), along_z(give_far, owners)

        p_squares = square_sum(p_all_a) + square_sum(p_all_b)
        sizes = [p_squares.shape[0], keep_a[0].shape[0], keep_a[1].shape[0]]
        squares = along_z(jnp.concatenate(
            [p_squares] + [square_sum(a) + square_sum(b) for a, b in zip(give_a, give_b)]
        ), owners)
        pool_var = 1.0 + (p_squares + squares[:sizes[0]])

        def log_sums(group, given, offset):
            a, b = keep_a[group], keep_b[group]
            target_var = 1.0 + (square_sum(a) + square_sum(b) + squares[offset:offset + sizes[1 + group]])
            cross = matmul_t(a, p_all_a) + matmul_t(b, p_all_b) + given
            ratio = jnp.square(cross) / (target_var[:, None] * pool_var[None, :])
            return -0.5 * jnp.sum(jnp.log1p(-ratio), axis=0)

        sums = log_sums(0, jnp.concatenate([given_near, given_side], axis=1), sizes[0])
        sums = sums + log_sums(1, given_far, sizes[0] + sizes[1])

        blocks = [sums[s * count:(s + 1) * count] for s in range(n_pool)]
        own = blocks[0] + along_z(blocks[0], owners)
        for s in range(1, n_pool):
            own = own + (over_pool(blocks[s], -s) + over_pool(blocks[s], -s, 0, owners))
        rows = [in_order([own if s == 0 else inner(own, s, 0), inner(own, s, 1)], core) for s in range(nx)]
        scores = in_order(rows, x)
        return jnp.where(z >= nz - 2, scores, along_z(scores, skip))

    return body


def solution(mesh):
    in_specs = (P("pool", "tgt"), P("pool"), P("pool", "tgt"), P("tgt", None))
    out_specs = P("pool")
    body = make_body(mesh.shape["pool"], mesh.shape["tgt"])
    return jax.shard_map(body, mesh=mesh, in_specs=in_specs, out_specs=out_specs, check_vma=False)
```

```python
import jax
import jax.numpy as jnp
from jax import lax
from jax.sharding import PartitionSpec as P

QUARTERS = 4
CORES = 2
BF = jnp.bfloat16
F32 = jnp.float32


def matmul(a, b):
    return lax.dot_general(a, b, (((1,), (0,)), ((), ())), preferred_element_type=F32)


def matmul_t(a, b):
    return lax.dot_general(a, b, (((1,), (1,)), ((), ())), preferred_element_type=F32)


def token(*arrays):
    width = min(v.shape[-1] for v in arrays)
    rows = [lax.slice_in_dim(v.reshape(-1, v.shape[-1])[:1], 0, width, axis=1) for v in arrays]
    return sum(jnp.minimum(jnp.abs(r.astype(F32)), 0.0) for r in rows)


def fence(first, second, others):
    done = lax.optimization_barrier(token(*first))
    done = lax.optimization_barrier(token(*second) + done)
    return token(*others) + done


def behind(value, zeros):
    zeros = zeros if zeros.shape[-1] == 1 else zeros[:, :value.shape[-1]]
    return value + zeros.astype(value.dtype)


def square_sum(a):
    return jnp.sum(jnp.square(a.astype(F32)), axis=1)


def make_body(n_pool, n_tgt):
    nz = QUARTERS
    nx = n_tgt // (nz * CORES)
    outer = (1, 0, 3, 2)
    owners = (0, 1, 3, 2)
    middle = (0, 2, 1, 3)
    skip = (2, 3, 0, 1)

    def place(z, x, c):
        return (z * nx + x) * CORES + c

    def inner(value, shift, flip):
        pairs = [
            (place(z, x, c), place(z, (x + shift) % nx, c ^ flip))
            for z in range(nz) for x in range(nx) for c in range(CORES)
        ]
        return lax.ppermute(value, "tgt", pairs)

    def along_z(value, to):
        pairs = [
            (place(z, x, c), place(to[z], x, c ^ (to[z] == z)))
            for z in range(nz) for x in range(nx) for c in range(CORES)
        ]
        return lax.ppermute(value, "tgt", pairs)

    def over_pool(value, shift, flip=0, to=None):
        to = to or range(nz)
        pairs = [
            (p * n_tgt + place(z, x, c), ((p + shift) % n_pool) * n_tgt + place(to[z], x, c ^ flip))
            for p in range(n_pool) for z in range(nz) for x in range(nx) for c in range(CORES)
        ]
        return lax.ppermute(value, ("pool", "tgt"), pairs)

    def in_order(pieces, index):
        n = len(pieces)
        if n == 2:
            low = index == 0
            return jnp.concatenate([jnp.where(low, pieces[0], pieces[1]), jnp.where(low, pieces[1], pieces[0])], axis=0)
        stacked = jnp.take(jnp.stack(pieces), (index - jnp.arange(n)) % n, axis=0)
        return stacked.reshape((-1,) + stacked.shape[2:])

    def choose(values, z):
        out = jnp.int32(values[0])
        for k in range(1, nz):
            out = jnp.where(z == k, jnp.int32(values[k]), out)
        return out

    def body(pool_table, pool_index, target_features, posterior_factor):
        me = lax.axis_index("tgt")
        core = me % CORES
        x = (me // CORES) % nx
        z = me // (CORES * nx)
        top = z == nz - 1
        width, hidden = posterior_factor.shape
        quarter = hidden // nz

        local_index = pool_index - lax.axis_index("pool") * pool_table.shape[0]
        pool_rows = pool_table.at[local_index].get(mode="promise_in_bounds")
        count = pool_rows.shape[0] // (nx * CORES)
        count_t = target_features.shape[0] // (nx * CORES)

        rows = jnp.concatenate([
            target_features.reshape(nx, CORES, count_t, width), pool_rows.reshape(nx, CORES, count, width)
        ], axis=2)
        n_rows = count + count_t

        def rows_of(s, f):
            return lax.dynamic_slice(rows, (lax.rem(x + s, nx), core ^ f, 0, 0), (1, 1, n_rows, width))[0, 0]

        def factor_own(choice):
            return lax.dynamic_slice_in_dim(posterior_factor, choose(choice, z) * quarter, quarter, 1)

        def factor_x(own):
            return [inner(own, s, 0) for s in range(1, nx)]

        def partial(pieces):
            total = None
            for f, l in zip(features, pieces):
                term = matmul(f, l)
                total = term if total is None else total + term
            return total

        def factor_flip(same):
            return [inner(v, 0, 1) for v in same]

        order = [(s, 0) for s in range(nx)] + [(s, 1) for s in range(nx)]

        own1 = lax.optimization_barrier(factor_own([0, 1, 2, 1]))
        same1 = [own1] + factor_x(own1)

        done = token(*same1[1:])
        features = [inner(behind(rows_of(s, f), done), s, f) if s or f else rows_of(0, 0) for s, f in order]
        first = partial(same1 + factor_flip(same1)).astype(BF)

        start = token(first)
        step1 = along_z(first, outer)
        step2 = along_z(first, middle)
        own2 = behind(factor_own([0, 0, 0, 0]), start)
        own3 = behind(factor_own([1, 1, 1, 2]), start)
        own4 = behind(factor_own([3, 3, 3, 3]), start)
        flip2, flip3, flip4 = inner(own2, 0, 1), inner(own3, 0, 1), inner(own4, 0, 1)
        moved2, moved3 = factor_x(own2), factor_x(own3)
        done = fence([step2, step1], [*moved2, *moved3], [flip2, flip3, flip4])
        moved2, moved3 = [behind(v, done) for v in moved2], [behind(v, done) for v in moved3]
        second = partial([own2] + moved2 + [flip2] + factor_flip(moved2))
        third = partial([own3] + moved3 + [flip3] + factor_flip(moved3))

        start = token(second, third) + done
        step3 = along_z(behind(second, start).astype(BF), owners)
        step4 = along_z((behind(second, start) + step1.astype(F32)).astype(BF), middle)
        white_a = (third + step1.astype(F32) + jnp.where(top, 0.0, step2.astype(F32)) + start).astype(BF)
        moved4 = factor_x(behind(own4, start))
        t_a, p_a = white_a[:count_t], white_a[count_t:]
        t_moved_a = [inner(t_a, s, 0) for s in range(1, nx)]
        p_moved_a = [over_pool(p_a, s) for s in range(1, n_pool)]
        done = fence([step3, step4], [*moved4, *t_moved_a], p_moved_a)

        moved4 = [behind(v, done) for v in moved4]
        fourth = partial([own4] + moved4 + [flip4] + factor_flip(moved4))
        t_moved_a = [behind(v, done) for v in t_moved_a]
        t_flip_a = inner(behind(t_a, done), 0, 1)
        white_b = (jnp.where(top, fourth, second + step3.astype(F32) + step4.astype(F32)) + done).astype(BF)
        t_b, p_b = white_b[:count_t], white_b[count_t:]
        t_moved_b = [inner(t_b, s, 0) for s in range(1, nx)]
        p_moved_b = [over_pool(p_b, s) for s in range(1, n_pool)]
        t_flip_b = inner(t_b, 0, 1)

        def groups(t, t_moved, t_flip):
            far, far_flip = jnp.concatenate(t_moved, axis=0), jnp.concatenate([inner(v, 0, 1) for v in t_moved], axis=0)
            keep = jnp.where(top, t_flip, t), jnp.where(top, far_flip, far)
            give = jnp.where(top, t, t_flip), jnp.where(top, far, far_flip)
            return keep, give

        keep_a, give_a = groups(t_a, t_moved_a, t_flip_a)
        keep_b, give_b = groups(t_b, t_moved_b, t_flip_b)
        p_far_a, p_far_b = jnp.concatenate(p_moved_a, axis=0), jnp.concatenate(p_moved_b, axis=0)
        p_all_a, p_all_b = jnp.concatenate([p_a, p_far_a], axis=0), jnp.concatenate([p_b, p_far_b], axis=0)

        given_near = along_z(matmul_t(give_a[0], p_a) + matmul_t(give_b[0], p_b), owners)
        swapped = token(given_near)
        swapped = swapped if p_far_a.shape[0] == p_a.shape[0] else swapped[:, :1]
        give_side = behind(matmul_t(give_a[0], p_far_a) + matmul_t(give_b[0], p_far_b), swapped)
        given_side = along_z(give_side, owners)
        given_far = along_z(matmul_t(give_a[1], p_all_a) + matmul_t(give_b[1], p_all_b), owners)

        p_squares = square_sum(p_all_a) + square_sum(p_all_b)
        sizes = [p_squares.shape[0], keep_a[0].shape[0], keep_a[1].shape[0]]
        squares = along_z(jnp.concatenate(
            [p_squares] + [square_sum(a) + square_sum(b) for a, b in zip(give_a, give_b)]
        ), owners)
        pool_var = 1.0 + (p_squares + squares[:sizes[0]])

        def log_sums(group, given, offset):
            a, b = keep_a[group], keep_b[group]
            target_var = 1.0 + (square_sum(a) + square_sum(b) + squares[offset:offset + sizes[1 + group]])
            cross = matmul_t(a, p_all_a) + matmul_t(b, p_all_b) + given
            ratio = jnp.square(cross) / (target_var[:, None] * pool_var[None, :])
            return -0.5 * jnp.sum(jnp.log1p(-ratio), axis=0)

        sums = log_sums(0, jnp.concatenate([given_near, given_side], axis=1), sizes[0])
        sums = sums + log_sums(1, given_far, sizes[0] + sizes[1])

        blocks = [sums[s * count:(s + 1) * count] for s in range(n_pool)]
        own = blocks[0] + along_z(blocks[0], owners)
        for s in range(1, n_pool):
            own = own + (over_pool(blocks[s], -s) + over_pool(blocks[s], -s, 0, owners))
        rows = [in_order([own if s == 0 else inner(own, s, 0), inner(own, s, 1)], core) for s in range(nx)]
        scores = in_order(rows, x)
        return jnp.where(z >= nz - 2, scores, along_z(scores, skip))

    return body


def solution(mesh):
    in_specs = (P("pool", "tgt"), P("pool"), P("pool", "tgt"), P("tgt", None))
    out_specs = P("pool")
    body = make_body(mesh.shape["pool"], mesh.shape["tgt"])
    return jax.shard_map(body, mesh=mesh, in_specs=in_specs, out_specs=out_specs, check_vma=False)
```

```python
import jax
import jax.numpy as jnp
from jax import lax
from jax.sharding import PartitionSpec as P

QUARTERS = 4
CORES = 2
BF = jnp.bfloat16
F32 = jnp.float32


def matmul(a, b):
    return lax.dot_general(a, b, (((1,), (0,)), ((), ())), preferred_element_type=F32)


def matmul_t(a, b):
    return lax.dot_general(a, b, (((1,), (1,)), ((), ())), preferred_element_type=F32)


def token(*arrays):
    width = min(v.shape[-1] for v in arrays)
    rows = [lax.slice_in_dim(v.reshape(-1, v.shape[-1])[:1], 0, width, axis=1) for v in arrays]
    return sum(jnp.minimum(jnp.abs(r.astype(F32)), 0.0) for r in rows)


def fence(first, second, others):
    done = lax.optimization_barrier(token(*first))
    done = lax.optimization_barrier(token(*second) + done)
    return token(*others) + done


def chained(zeros, steps):
    for _ in range(steps):
        zeros = lax.optimization_barrier(jnp.minimum(jnp.abs(zeros), 0.0))
    return zeros


def behind(value, zeros):
    zeros = zeros if zeros.shape[-1] == 1 else zeros[:, :value.shape[-1]]
    return value + zeros.astype(value.dtype)


def square_sum(a):
    return jnp.sum(jnp.square(a.astype(F32)), axis=1)


def make_body(n_pool, n_tgt):
    nz = QUARTERS
    nx = n_tgt // (nz * CORES)
    outer = (1, 0, 3, 2)
    owners = (0, 1, 3, 2)
    middle = (0, 2, 1, 3)
    skip = (2, 3, 0, 1)

    def place(z, x, c):
        return (z * nx + x) * CORES + c

    def inner(value, shift, flip):
        pairs = [
            (place(z, x, c), place(z, (x + shift) % nx, c ^ flip))
            for z in range(nz) for x in range(nx) for c in range(CORES)
        ]
        return lax.ppermute(value, "tgt", pairs)

    def along_z(value, to):
        pairs = [
            (place(z, x, c), place(to[z], x, c ^ (to[z] == z)))
            for z in range(nz) for x in range(nx) for c in range(CORES)
        ]
        return lax.ppermute(value, "tgt", pairs)

    def over_pool(value, shift, flip=0, to=None):
        to = to or range(nz)
        pairs = [
            (p * n_tgt + place(z, x, c), ((p + shift) % n_pool) * n_tgt + place(to[z], x, c ^ flip))
            for p in range(n_pool) for z in range(nz) for x in range(nx) for c in range(CORES)
        ]
        return lax.ppermute(value, ("pool", "tgt"), pairs)

    def in_order(pieces, index):
        n = len(pieces)
        if n == 2:
            low = index == 0
            return jnp.concatenate([jnp.where(low, pieces[0], pieces[1]), jnp.where(low, pieces[1], pieces[0])], axis=0)
        stacked = jnp.take(jnp.stack(pieces), (index - jnp.arange(n)) % n, axis=0)
        return stacked.reshape((-1,) + stacked.shape[2:])

    def choose(values, z):
        out = jnp.int32(values[0])
        for k in range(1, nz):
            out = jnp.where(z == k, jnp.int32(values[k]), out)
        return out

    def body(pool_table, pool_index, target_features, posterior_factor):
        me = lax.axis_index("tgt")
        core = me % CORES
        x = (me // CORES) % nx
        z = me // (CORES * nx)
        top = z == nz - 1
        width, hidden = posterior_factor.shape
        quarter = hidden // nz

        local_index = pool_index - lax.axis_index("pool") * pool_table.shape[0]
        pool_rows = pool_table.at[local_index].get(mode="promise_in_bounds")
        count = pool_rows.shape[0] // (nx * CORES)
        count_t = target_features.shape[0] // (nx * CORES)

        rows = jnp.concatenate([
            target_features.reshape(nx, CORES, count_t, width), pool_rows.reshape(nx, CORES, count, width)
        ], axis=2)
        n_rows = count + count_t

        def rows_of(s, f):
            return lax.dynamic_slice(rows, (lax.rem(x + s, nx), core ^ f, 0, 0), (1, 1, n_rows, width))[0, 0]

        def factor_own(choice):
            return lax.dynamic_slice_in_dim(posterior_factor, choose(choice, z) * quarter, quarter, 1)

        def factor_x(own):
            return [inner(own, s, 0) for s in range(1, nx)]

        def partial(pieces):
            total = None
            for f, l in zip(features, pieces):
                term = matmul(f, l)
                total = term if total is None else total + term
            return total

        def factor_flip(same):
            return [inner(v, 0, 1) for v in same]

        order = [(s, 0) for s in range(nx)] + [(s, 1) for s in range(nx)]

        own1 = lax.optimization_barrier(factor_own([0, 1, 2, 1]))
        moved1 = factor_x(own1)
        arrived = chained(token(*moved1), 4)

        features = [inner(rows_of(s, f), s, f) if s or f else rows_of(0, 0) for s, f in order]
        same1 = [own1] + [behind(v, arrived) for v in moved1]
        first = partial(same1 + factor_flip(same1)).astype(BF)

        start = token(first)
        step1 = along_z(first, outer)
        step2 = along_z(first, middle)
        own2 = behind(factor_own([0, 0, 0, 0]), start)
        own3 = behind(factor_own([1, 1, 1, 2]), start)
        own4 = behind(factor_own([3, 3, 3, 3]), start)
        flip2, flip3, flip4 = inner(own2, 0, 1), inner(own3, 0, 1), inner(own4, 0, 1)
        moved2, moved3 = factor_x(own2), factor_x(own3)
        done = fence([step2, step1], [*moved2, *moved3], [flip2, flip3, flip4])
        moved2, moved3 = [behind(v, done) for v in moved2], [behind(v, done) for v in moved3]
        second = partial([own2] + moved2 + [flip2] + factor_flip(moved2))
        third = partial([own3] + moved3 + [flip3] + factor_flip(moved3))

        start = token(second, third) + done
        step3 = along_z(behind(second, start).astype(BF), owners)
        step4 = along_z((behind(second, start) + step1.astype(F32)).astype(BF), middle)
        white_a = (third + step1.astype(F32) + jnp.where(top, 0.0, step2.astype(F32)) + start).astype(BF)
        moved4 = factor_x(behind(own4, start))
        t_a, p_a = white_a[:count_t], white_a[count_t:]
        t_moved_a = [inner(t_a, s, 0) for s in range(1, nx)]
        p_moved_a = [over_pool(p_a, s) for s in range(1, n_pool)]
        done = fence([step3, step4], [*moved4, *t_moved_a], p_moved_a)

        moved4 = [behind(v, done) for v in moved4]
        fourth = partial([own4] + moved4 + [flip4] + factor_flip(moved4))
        t_moved_a = [behind(v, done) for v in t_moved_a]
        t_flip_a = inner(behind(t_a, done), 0, 1)
        white_b = (jnp.where(top, fourth, second + step3.astype(F32) + step4.astype(F32)) + done).astype(BF)
        t_b, p_b = white_b[:count_t], white_b[count_t:]
        t_moved_b = [inner(t_b, s, 0) for s in range(1, nx)]
        p_moved_b = [over_pool(p_b, s) for s in range(1, n_pool)]
        t_flip_b = inner(t_b, 0, 1)

        def groups(t, t_moved, t_flip):
            far, far_flip = jnp.concatenate(t_moved, axis=0), jnp.concatenate([inner(v, 0, 1) for v in t_moved], axis=0)
            keep = jnp.where(top, t_flip, t), jnp.where(top, far_flip, far)
            give = jnp.where(top, t, t_flip), jnp.where(top, far, far_flip)
            return keep, give

        keep_a, give_a = groups(t_a, t_moved_a, t_flip_a)
        keep_b, give_b = groups(t_b, t_moved_b, t_flip_b)
        p_far_a, p_far_b = jnp.concatenate(p_moved_a, axis=0), jnp.concatenate(p_moved_b, axis=0)
        p_all_a, p_all_b = jnp.concatenate([p_a, p_far_a], axis=0), jnp.concatenate([p_b, p_far_b], axis=0)

        given_near = along_z(matmul_t(give_a[0], p_a) + matmul_t(give_b[0], p_b), owners)
        swapped = token(given_near)
        swapped = swapped if p_far_a.shape[0] == p_a.shape[0] else swapped[:, :1]
        give_side = behind(matmul_t(give_a[0], p_far_a) + matmul_t(give_b[0], p_far_b), swapped)
        given_side = along_z(give_side, owners)
        given_far = along_z(matmul_t(give_a[1], p_all_a) + matmul_t(give_b[1], p_all_b), owners)

        p_squares = square_sum(p_all_a) + square_sum(p_all_b)
        sizes = [p_squares.shape[0], keep_a[0].shape[0], keep_a[1].shape[0]]
        squares = along_z(jnp.concatenate(
            [p_squares] + [square_sum(a) + square_sum(b) for a, b in zip(give_a, give_b)]
        ), owners)
        pool_var = 1.0 + (p_squares + squares[:sizes[0]])

        def log_sums(group, given, offset):
            a, b = keep_a[group], keep_b[group]
            target_var = 1.0 + (square_sum(a) + square_sum(b) + squares[offset:offset + sizes[1 + group]])
            cross = matmul_t(a, p_all_a) + matmul_t(b, p_all_b) + given
            ratio = jnp.square(cross) / (target_var[:, None] * pool_var[None, :])
            return -0.5 * jnp.sum(jnp.log1p(-ratio), axis=0)

        sums = log_sums(0, jnp.concatenate([given_near, given_side], axis=1), sizes[0])
        sums = sums + log_sums(1, given_far, sizes[0] + sizes[1])

        blocks = [sums[s * count:(s + 1) * count] for s in range(n_pool)]
        own = blocks[0] + along_z(blocks[0], owners)
        for s in range(1, n_pool):
            own = own + (over_pool(blocks[s], -s) + over_pool(blocks[s], -s, 0, owners))
        rows = [in_order([own if s == 0 else inner(own, s, 0), inner(own, s, 1)], core) for s in range(nx)]
        scores = in_order(rows, x)
        return jnp.where(z >= nz - 2, scores, along_z(scores, skip))

    return body


def solution(mesh):
    in_specs = (P("pool", "tgt"), P("pool"), P("pool", "tgt"), P("tgt", None))
    out_specs = P("pool")
    body = make_body(mesh.shape["pool"], mesh.shape["tgt"])
    return jax.shard_map(body, mesh=mesh, in_specs=in_specs, out_specs=out_specs, check_vma=False)
```

```python
import jax
import jax.numpy as jnp
from jax import lax
from jax.sharding import PartitionSpec as P

QUARTERS = 4
CORES = 2
BF = jnp.bfloat16
F32 = jnp.float32


def matmul(a, b):
    return lax.dot_general(a, b, (((1,), (0,)), ((), ())), preferred_element_type=F32)


def matmul_t(a, b):
    return lax.dot_general(a, b, (((1,), (1,)), ((), ())), preferred_element_type=F32)


def token(*arrays):
    width = min(v.shape[-1] for v in arrays)
    rows = [lax.slice_in_dim(v.reshape(-1, v.shape[-1])[:1], 0, width, axis=1) for v in arrays]
    return sum(jnp.minimum(jnp.abs(r.astype(F32)), 0.0) for r in rows)


def fence(first, second, others):
    done = lax.optimization_barrier(token(*first))
    done = lax.optimization_barrier(token(*second) + done)
    return token(*others) + done


def chained(zeros, steps):
    for _ in range(steps):
        zeros = lax.optimization_barrier(jnp.minimum(jnp.abs(zeros), 0.0))
    return zeros


def behind(value, zeros):
    zeros = zeros if zeros.shape[-1] == 1 else zeros[:, :value.shape[-1]]
    return value + zeros.astype(value.dtype)


def square_sum(a):
    return jnp.sum(jnp.square(a.astype(F32)), axis=1)


def make_body(n_pool, n_tgt):
    nz = QUARTERS
    nx = n_tgt // (nz * CORES)
    outer = (1, 0, 3, 2)
    owners = (0, 1, 3, 2)
    middle = (0, 2, 1, 3)
    skip = (2, 3, 0, 1)

    def place(z, x, c):
        return (z * nx + x) * CORES + c

    def inner(value, shift, flip):
        pairs = [
            (place(z, x, c), place(z, (x + shift) % nx, c ^ flip))
            for z in range(nz) for x in range(nx) for c in range(CORES)
        ]
        return lax.ppermute(value, "tgt", pairs)

    def along_z(value, to):
        pairs = [
            (place(z, x, c), place(to[z], x, c ^ (to[z] == z)))
            for z in range(nz) for x in range(nx) for c in range(CORES)
        ]
        return lax.ppermute(value, "tgt", pairs)

    def over_pool(value, shift, flip=0, to=None):
        to = to or range(nz)
        pairs = [
            (p * n_tgt + place(z, x, c), ((p + shift) % n_pool) * n_tgt + place(to[z], x, c ^ flip))
            for p in range(n_pool) for z in range(nz) for x in range(nx) for c in range(CORES)
        ]
        return lax.ppermute(value, ("pool", "tgt"), pairs)

    def in_order(pieces, index):
        n = len(pieces)
        if n == 2:
            low = index == 0
            return jnp.concatenate([jnp.where(low, pieces[0], pieces[1]), jnp.where(low, pieces[1], pieces[0])], axis=0)
        stacked = jnp.take(jnp.stack(pieces), (index - jnp.arange(n)) % n, axis=0)
        return stacked.reshape((-1,) + stacked.shape[2:])

    def choose(values, z):
        out = jnp.int32(values[0])
        for k in range(1, nz):
            out = jnp.where(z == k, jnp.int32(values[k]), out)
        return out

    def body(pool_table, pool_index, target_features, posterior_factor):
        me = lax.axis_index("tgt")
        core = me % CORES
        x = (me // CORES) % nx
        z = me // (CORES * nx)
        top = z == nz - 1
        width, hidden = posterior_factor.shape
        quarter = hidden // nz

        local_index = pool_index - lax.axis_index("pool") * pool_table.shape[0]
        pool_rows = pool_table.at[local_index].get(mode="promise_in_bounds")
        count = pool_rows.shape[0] // (nx * CORES)
        count_t = target_features.shape[0] // (nx * CORES)

        rows = jnp.concatenate([
            target_features.reshape(nx, CORES, count_t, width), pool_rows.reshape(nx, CORES, count, width)
        ], axis=2)
        n_rows = count + count_t

        def rows_of(s, f):
            return lax.dynamic_slice(rows, (lax.rem(x + s, nx), core ^ f, 0, 0), (1, 1, n_rows, width))[0, 0]

        def factor_own(choice):
            return lax.dynamic_slice_in_dim(posterior_factor, choose(choice, z) * quarter, quarter, 1)

        def factor_x(own):
            return [inner(own, s, 0) for s in range(1, nx)]

        def partial(pieces):
            total = None
            for f, l in zip(features, pieces):
                term = matmul(f, l)
                total = term if total is None else total + term
            return total

        def factor_flip(same):
            return [inner(v, 0, 1) for v in same]

        order = [(s, 0) for s in range(nx)] + [(s, 1) for s in range(nx)]

        own1 = lax.optimization_barrier(factor_own([0, 1, 2, 1]))
        moved1 = factor_x(own1)
        arrived = chained(token(*moved1), 4)

        features = [inner(rows_of(s, f), s, f) if s or f else rows_of(0, 0) for s, f in order]
        same1 = [own1] + [behind(v, arrived) for v in moved1]
        first = partial(same1 + factor_flip(same1)).astype(BF)

        start = token(first)
        step1 = along_z(first, outer)
        step2 = along_z(first, middle)
        own2 = behind(factor_own([0, 0, 0, 0]), start)
        own3 = behind(factor_own([1, 1, 1, 2]), start)
        own4 = behind(factor_own([3, 3, 3, 3]), start)
        flip2, flip3, flip4 = inner(own2, 0, 1), inner(own3, 0, 1), inner(own4, 0, 1)
        moved2, moved3 = factor_x(own2), factor_x(own3)
        done = fence([step2, step1], [*moved2, *moved3], [flip2, flip3, flip4])
        moved2, moved3 = [behind(v, done) for v in moved2], [behind(v, done) for v in moved3]
        second = partial([own2] + moved2 + [flip2] + factor_flip(moved2))
        third = partial([own3] + moved3 + [flip3] + factor_flip(moved3))

        start = token(second, third) + done
        step3 = along_z(behind(second, start).astype(BF), owners)
        step4 = along_z((behind(second, start) + step1.astype(F32)).astype(BF), middle)
        white_a = (third + step1.astype(F32) + jnp.where(top, 0.0, step2.astype(F32)) + start).astype(BF)
        moved4 = factor_x(behind(own4, start))
        t_a, p_a = white_a[:count_t], white_a[count_t:]
        t_moved_a = [inner(t_a, s, 0) for s in range(1, nx)]
        p_moved_a = [over_pool(p_a, s) for s in range(1, n_pool)]
        far4 = factor_flip(moved4)
        done = fence([step3, step4], [*t_moved_a, *p_moved_a], far4)

        fourth = partial([own4] + moved4 + [flip4] + far4)
        t_moved_a = [behind(v, done) for v in t_moved_a]
        t_flip_a = inner(behind(t_a, done), 0, 1)
        white_b = (jnp.where(top, fourth, second + step3.astype(F32) + step4.astype(F32)) + done).astype(BF)
        t_b, p_b = white_b[:count_t], white_b[count_t:]
        t_moved_b = [inner(t_b, s, 0) for s in range(1, nx)]
        p_moved_b = [over_pool(p_b, s) for s in range(1, n_pool)]
        t_flip_b = inner(t_b, 0, 1)

        def groups(t, t_moved, t_flip):
            far, far_flip = jnp.concatenate(t_moved, axis=0), jnp.concatenate([inner(v, 0, 1) for v in t_moved], axis=0)
            keep = jnp.where(top, t_flip, t), jnp.where(top, far_flip, far)
            give = jnp.where(top, t, t_flip), jnp.where(top, far, far_flip)
            return keep, give

        keep_a, give_a = groups(t_a, t_moved_a, t_flip_a)
        keep_b, give_b = groups(t_b, t_moved_b, t_flip_b)
        p_far_a, p_far_b = jnp.concatenate(p_moved_a, axis=0), jnp.concatenate(p_moved_b, axis=0)
        p_all_a, p_all_b = jnp.concatenate([p_a, p_far_a], axis=0), jnp.concatenate([p_b, p_far_b], axis=0)

        given_near = along_z(matmul_t(give_a[0], p_a) + matmul_t(give_b[0], p_b), owners)
        swapped = token(given_near)
        swapped = swapped if p_far_a.shape[0] == p_a.shape[0] else swapped[:, :1]
        give_side = behind(matmul_t(give_a[0], p_far_a) + matmul_t(give_b[0], p_far_b), swapped)
        given_side = along_z(give_side, owners)
        given_far = along_z(matmul_t(give_a[1], p_all_a) + matmul_t(give_b[1], p_all_b), owners)

        p_squares = square_sum(p_all_a) + square_sum(p_all_b)
        sizes = [p_squares.shape[0], keep_a[0].shape[0], keep_a[1].shape[0]]
        squares = along_z(jnp.concatenate(
            [p_squares] + [square_sum(a) + square_sum(b) for a, b in zip(give_a, give_b)]
        ), owners)
        pool_var = 1.0 + (p_squares + squares[:sizes[0]])

        def log_sums(group, given, offset):
            a, b = keep_a[group], keep_b[group]
            target_var = 1.0 + (square_sum(a) + square_sum(b) + squares[offset:offset + sizes[1 + group]])
            cross = matmul_t(a, p_all_a) + matmul_t(b, p_all_b) + given
            ratio = jnp.square(cross) / (target_var[:, None] * pool_var[None, :])
            return -0.5 * jnp.sum(jnp.log1p(-ratio), axis=0)

        sums = log_sums(0, jnp.concatenate([given_near, given_side], axis=1), sizes[0])
        sums = sums + log_sums(1, given_far, sizes[0] + sizes[1])

        blocks = [sums[s * count:(s + 1) * count] for s in range(n_pool)]
        own = blocks[0] + along_z(blocks[0], owners)
        for s in range(1, n_pool):
            own = own + (over_pool(blocks[s], -s) + over_pool(blocks[s], -s, 0, owners))
        rows = [in_order([own if s == 0 else inner(own, s, 0), inner(own, s, 1)], core) for s in range(nx)]
        scores = in_order(rows, x)
        return jnp.where(z >= nz - 2, scores, along_z(scores, skip))

    return body


def solution(mesh):
    in_specs = (P("pool", "tgt"), P("pool"), P("pool", "tgt"), P("tgt", None))
    out_specs = P("pool")
    body = make_body(mesh.shape["pool"], mesh.shape["tgt"])
    return jax.shard_map(body, mesh=mesh, in_specs=in_specs, out_specs=out_specs, check_vma=False)
```

```python
import jax
import jax.numpy as jnp
from jax import lax
from jax.sharding import PartitionSpec as P

QUARTERS = 4
CORES = 2
BF = jnp.bfloat16
F32 = jnp.float32


def matmul(a, b):
    return lax.dot_general(a, b, (((1,), (0,)), ((), ())), preferred_element_type=F32)


def matmul_t(a, b):
    return lax.dot_general(a, b, (((1,), (1,)), ((), ())), preferred_element_type=F32)


def token(*arrays):
    width = min(v.shape[-1] for v in arrays)
    rows = [lax.slice_in_dim(v.reshape(-1, v.shape[-1])[:1], 0, width, axis=1) for v in arrays]
    return sum(jnp.minimum(jnp.abs(r.astype(F32)), 0.0) for r in rows)


def fence(first, second, others):
    done = lax.optimization_barrier(token(*first))
    done = lax.optimization_barrier(token(*second) + done)
    return token(*others) + done


def chained(zeros, steps):
    for _ in range(steps):
        zeros = lax.optimization_barrier(jnp.minimum(jnp.abs(zeros), 0.0))
    return zeros


def behind(value, zeros):
    zeros = zeros if zeros.shape[-1] == 1 else zeros[:, :value.shape[-1]]
    return value + zeros.astype(value.dtype)


def square_sum(a):
    return jnp.sum(jnp.square(a.astype(F32)), axis=1)


def make_body(n_pool, n_tgt):
    nz = QUARTERS
    nx = n_tgt // (nz * CORES)
    outer = (1, 0, 3, 2)
    owners = (0, 1, 3, 2)
    middle = (0, 2, 1, 3)
    skip = (2, 3, 0, 1)

    def place(z, x, c):
        return (z * nx + x) * CORES + c

    def inner(value, shift, flip):
        pairs = [
            (place(z, x, c), place(z, (x + shift) % nx, c ^ flip))
            for z in range(nz) for x in range(nx) for c in range(CORES)
        ]
        return lax.ppermute(value, "tgt", pairs)

    def along_z(value, to):
        pairs = [
            (place(z, x, c), place(to[z], x, c ^ (to[z] == z)))
            for z in range(nz) for x in range(nx) for c in range(CORES)
        ]
        return lax.ppermute(value, "tgt", pairs)

    def over_pool(value, shift, flip=0, to=None):
        to = to or range(nz)
        pairs = [
            (p * n_tgt + place(z, x, c), ((p + shift) % n_pool) * n_tgt + place(to[z], x, c ^ flip))
            for p in range(n_pool) for z in range(nz) for x in range(nx) for c in range(CORES)
        ]
        return lax.ppermute(value, ("pool", "tgt"), pairs)

    def in_order(pieces, index):
        n = len(pieces)
        if n == 2:
            low = index == 0
            return jnp.concatenate([jnp.where(low, pieces[0], pieces[1]), jnp.where(low, pieces[1], pieces[0])], axis=0)
        stacked = jnp.take(jnp.stack(pieces), (index - jnp.arange(n)) % n, axis=0)
        return stacked.reshape((-1,) + stacked.shape[2:])

    def choose(values, z):
        out = jnp.int32(values[0])
        for k in range(1, nz):
            out = jnp.where(z == k, jnp.int32(values[k]), out)
        return out

    def body(pool_table, pool_index, target_features, posterior_factor):
        me = lax.axis_index("tgt")
        core = me % CORES
        x = (me // CORES) % nx
        z = me // (CORES * nx)
        top = z == nz - 1
        width, hidden = posterior_factor.shape
        quarter = hidden // nz

        local_index = pool_index - lax.axis_index("pool") * pool_table.shape[0]
        pool_rows = pool_table.at[local_index].get(mode="promise_in_bounds")
        count = pool_rows.shape[0] // (nx * CORES)
        count_t = target_features.shape[0] // (nx * CORES)

        rows = jnp.concatenate([
            target_features.reshape(nx, CORES, count_t, width), pool_rows.reshape(nx, CORES, count, width)
        ], axis=2)
        n_rows = count + count_t

        def rows_of(s, f):
            return lax.dynamic_slice(rows, (lax.rem(x + s, nx), core ^ f, 0, 0), (1, 1, n_rows, width))[0, 0]

        def factor_own(choice):
            return lax.dynamic_slice_in_dim(posterior_factor, choose(choice, z) * quarter, quarter, 1)

        def factor_x(own):
            return [inner(own, s, 0) for s in range(1, nx)]

        def partial(pieces):
            total = None
            for f, l in zip(features, pieces):
                term = matmul(f, l)
                total = term if total is None else total + term
            return total

        def factor_flip(same):
            return [inner(v, 0, 1) for v in same]

        order = [(s, 0) for s in range(nx)] + [(s, 1) for s in range(nx)]

        own1 = lax.optimization_barrier(factor_own([0, 1, 2, 1]))
        moved1 = factor_x(own1)
        arrived = chained(token(*moved1), 4)

        features = [inner(rows_of(s, f), s, f) if s or f else rows_of(0, 0) for s, f in order]
        same1 = [own1] + [behind(v, arrived) for v in moved1]
        first = partial(same1 + factor_flip(same1)).astype(BF)

        start = token(first)
        step1 = along_z(first, outer)
        step2 = along_z(first, middle)
        own2 = behind(factor_own([0, 0, 0, 0]), start)
        own3 = behind(factor_own([1, 1, 1, 2]), start)
        own4 = behind(factor_own([3, 3, 3, 3]), start)
        flip2, flip3, flip4 = inner(own2, 0, 1), inner(own3, 0, 1), inner(own4, 0, 1)
        moved2, moved3 = factor_x(own2), factor_x(own3)
        done = fence([step2, step1], [*moved2, *moved3], [flip2, flip3, flip4])
        moved2, moved3 = [behind(v, done) for v in moved2], [behind(v, done) for v in moved3]
        second = partial([own2] + moved2 + [flip2] + factor_flip(moved2))
        third = partial([own3] + moved3 + [flip3] + factor_flip(moved3))

        start = token(second, third) + done
        step3 = along_z(behind(second, start).astype(BF), owners)
        step4 = along_z((behind(second, start) + step1.astype(F32)).astype(BF), middle)
        white_a = (third + step1.astype(F32) + jnp.where(top, 0.0, step2.astype(F32)) + start).astype(BF)
        moved4 = factor_x(behind(own4, start))
        t_a, p_a = white_a[:count_t], white_a[count_t:]
        t_moved_a = [inner(t_a, s, 0) for s in range(1, nx)]
        p_moved_a = [over_pool(p_a, s) for s in range(1, n_pool)]
        far4 = factor_flip(moved4)
        done = fence([step3, step4], [*t_moved_a, *p_moved_a], far4)

        fourth = partial([own4] + moved4 + [flip4] + far4)
        t_moved_a = [behind(v, done) for v in t_moved_a]
        t_flip_a = inner(behind(t_a, done), 0, 1)
        white_b = (jnp.where(top, fourth, second + step3.astype(F32) + step4.astype(F32)) + done).astype(BF)
        t_b, p_b = white_b[:count_t], white_b[count_t:]
        t_moved_b = [inner(t_b, s, 0) for s in range(1, nx)]
        p_moved_b = [over_pool(p_b, s) for s in range(1, n_pool)]
        t_flip_b = inner(t_b, 0, 1)

        def groups(t, t_moved, t_flip):
            far, far_flip = jnp.concatenate(t_moved, axis=0), jnp.concatenate([inner(v, 0, 1) for v in t_moved], axis=0)
            keep = jnp.where(top, t_flip, t), jnp.where(top, far_flip, far)
            give = jnp.where(top, t, t_flip), jnp.where(top, far, far_flip)
            return keep, give

        keep_a, give_a = groups(t_a, t_moved_a, t_flip_a)
        keep_b, give_b = groups(t_b, t_moved_b, t_flip_b)
        p_far_a, p_far_b = jnp.concatenate(p_moved_a, axis=0), jnp.concatenate(p_moved_b, axis=0)
        p_all_a, p_all_b = jnp.concatenate([p_a, p_far_a], axis=0), jnp.concatenate([p_b, p_far_b], axis=0)

        given_near = along_z(matmul_t(give_a[0], p_a) + matmul_t(give_b[0], p_b), owners)
        swapped = token(given_near)
        swapped = swapped if p_far_a.shape[0] == p_a.shape[0] else swapped[:, :1]
        give_side = behind(matmul_t(give_a[0], p_far_a) + matmul_t(give_b[0], p_far_b), swapped)
        given_side = along_z(give_side, owners)
        given_far = along_z(matmul_t(give_a[1], p_all_a) + matmul_t(give_b[1], p_all_b), owners)

        p_squares = square_sum(p_all_a) + square_sum(p_all_b)
        sizes = [p_squares.shape[0], keep_a[0].shape[0], keep_a[1].shape[0]]
        squares = along_z(jnp.concatenate(
            [p_squares] + [square_sum(a) + square_sum(b) for a, b in zip(give_a, give_b)]
        ), owners)
        pool_var = 1.0 + (p_squares + squares[:sizes[0]])

        hold = token(given_side)[:, :1]

        def log_sums(group, given, offset):
            a, b = behind(keep_a[group], hold), behind(keep_b[group], hold)
            target_var = 1.0 + (square_sum(a) + square_sum(b) + squares[offset:offset + sizes[1 + group]])
            cross = matmul_t(a, p_all_a) + matmul_t(b, p_all_b) + given
            ratio = jnp.square(cross) / (target_var[:, None] * pool_var[None, :])
            return -0.5 * jnp.sum(jnp.log1p(-ratio), axis=0)

        sums = log_sums(0, jnp.concatenate([given_near, given_side], axis=1), sizes[0])
        sums = sums + log_sums(1, given_far, sizes[0] + sizes[1])

        blocks = [sums[s * count:(s + 1) * count] for s in range(n_pool)]
        own = blocks[0] + along_z(blocks[0], owners)
        for s in range(1, n_pool):
            own = own + (over_pool(blocks[s], -s) + over_pool(blocks[s], -s, 0, owners))
        rows = [in_order([own if s == 0 else inner(own, s, 0), inner(own, s, 1)], core) for s in range(nx)]
        scores = in_order(rows, x)
        return jnp.where(z >= nz - 2, scores, along_z(scores, skip))

    return body


def solution(mesh):
    in_specs = (P("pool", "tgt"), P("pool"), P("pool", "tgt"), P("tgt", None))
    out_specs = P("pool")
    body = make_body(mesh.shape["pool"], mesh.shape["tgt"])
    return jax.shard_map(body, mesh=mesh, in_specs=in_specs, out_specs=out_specs, check_vma=False)
```

```python
import jax
import jax.numpy as jnp
from jax import lax
from jax.sharding import PartitionSpec as P

QUARTERS = 4
CORES = 2
BF = jnp.bfloat16
F32 = jnp.float32


def matmul(a, b):
    return lax.dot_general(a, b, (((1,), (0,)), ((), ())), preferred_element_type=F32)


def matmul_t(a, b):
    return lax.dot_general(a, b, (((1,), (1,)), ((), ())), preferred_element_type=F32)


def token(*arrays):
    width = min(v.shape[-1] for v in arrays)
    rows = [lax.slice_in_dim(v.reshape(-1, v.shape[-1])[:1], 0, width, axis=1) for v in arrays]
    return sum(jnp.minimum(jnp.abs(r.astype(F32)), 0.0) for r in rows)


def fence(first, second, others):
    done = lax.optimization_barrier(token(*first))
    done = lax.optimization_barrier(token(*second) + done)
    return token(*others) + done


def chained(zeros, steps):
    for _ in range(steps):
        zeros = lax.optimization_barrier(jnp.minimum(jnp.abs(zeros), 0.0))
    return zeros


def behind(value, zeros):
    zeros = zeros if zeros.shape[-1] == 1 else zeros[:, :value.shape[-1]]
    return value + zeros.astype(value.dtype)


def square_sum(a):
    return jnp.sum(jnp.square(a.astype(F32)), axis=1)


def make_body(n_pool, n_tgt):
    nz = QUARTERS
    nx = n_tgt // (nz * CORES)
    outer = (1, 0, 3, 2)
    owners = (0, 1, 3, 2)
    middle = (0, 2, 1, 3)
    skip = (2, 3, 0, 1)

    def place(z, x, c):
        return (z * nx + x) * CORES + c

    def inner(value, shift, flip):
        pairs = [
            (place(z, x, c), place(z, (x + shift) % nx, c ^ flip))
            for z in range(nz) for x in range(nx) for c in range(CORES)
        ]
        return lax.ppermute(value, "tgt", pairs)

    def along_z(value, to):
        pairs = [
            (place(z, x, c), place(to[z], x, c ^ (to[z] == z)))
            for z in range(nz) for x in range(nx) for c in range(CORES)
        ]
        return lax.ppermute(value, "tgt", pairs)

    def over_pool(value, shift, flip=0, to=None):
        to = to or range(nz)
        pairs = [
            (p * n_tgt + place(z, x, c), ((p + shift) % n_pool) * n_tgt + place(to[z], x, c ^ flip))
            for p in range(n_pool) for z in range(nz) for x in range(nx) for c in range(CORES)
        ]
        return lax.ppermute(value, ("pool", "tgt"), pairs)

    def in_order(pieces, index):
        n = len(pieces)
        if n == 2:
            low = index == 0
            return jnp.concatenate([jnp.where(low, pieces[0], pieces[1]), jnp.where(low, pieces[1], pieces[0])], axis=0)
        stacked = jnp.take(jnp.stack(pieces), (index - jnp.arange(n)) % n, axis=0)
        return stacked.reshape((-1,) + stacked.shape[2:])

    def choose(values, z):
        out = jnp.int32(values[0])
        for k in range(1, nz):
            out = jnp.where(z == k, jnp.int32(values[k]), out)
        return out

    def body(pool_table, pool_index, target_features, posterior_factor):
        me = lax.axis_index("tgt")
        core = me % CORES
        x = (me // CORES) % nx
        z = me // (CORES * nx)
        top = z == nz - 1
        width, hidden = posterior_factor.shape
        quarter = hidden // nz

        local_index = pool_index - lax.axis_index("pool") * pool_table.shape[0]
        pool_rows = pool_table.at[local_index].get(mode="promise_in_bounds")
        count = pool_rows.shape[0] // (nx * CORES)
        count_t = target_features.shape[0] // (nx * CORES)

        rows = jnp.concatenate([
            target_features.reshape(nx, CORES, count_t, width), pool_rows.reshape(nx, CORES, count, width)
        ], axis=2)
        n_rows = count + count_t

        def rows_of(s, f):
            return lax.dynamic_slice(rows, (lax.rem(x + s, nx), core ^ f, 0, 0), (1, 1, n_rows, width))[0, 0]

        def factor_own(choice):
            return lax.dynamic_slice_in_dim(posterior_factor, choose(choice, z) * quarter, quarter, 1)

        def factor_x(own):
            return [inner(own, s, 0) for s in range(1, nx)]

        def partial(pieces):
            total = None
            for f, l in zip(features, pieces):
                term = matmul(f, l)
                total = term if total is None else total + term
            return total

        def factor_flip(same):
            return [inner(v, 0, 1) for v in same]

        order = [(s, 0) for s in range(nx)] + [(s, 1) for s in range(nx)]

        own1 = lax.optimization_barrier(factor_own([0, 1, 2, 1]))
        moved1 = factor_x(own1)
        arrived = chained(token(*moved1), 4)

        features = [inner(rows_of(s, f), s, f) if s or f else rows_of(0, 0) for s, f in order]
        same1 = [own1] + [behind(v, arrived) for v in moved1]
        first = partial(same1 + factor_flip(same1)).astype(BF)

        start = token(first)
        step1 = along_z(first, outer)
        step2 = along_z(first, middle)
        own2 = behind(factor_own([0, 0, 0, 0]), start)
        own3 = behind(factor_own([1, 1, 1, 2]), start)
        own4 = behind(factor_own([3, 3, 3, 3]), start)
        flip2, flip3, flip4 = inner(own2, 0, 1), inner(own3, 0, 1), inner(own4, 0, 1)
        moved2, moved3 = factor_x(own2), factor_x(own3)
        far2 = factor_flip(moved2)
        done = fence([step2, step1], moved3, [flip2, flip3, flip4, *far2])
        moved3 = [behind(v, done) for v in moved3]
        second = partial([own2] + moved2 + [flip2] + far2)
        third = partial([own3] + moved3 + [flip3] + factor_flip(moved3))

        start = token(second, third) + done
        step3 = along_z(behind(second, start).astype(BF), owners)
        step4 = along_z((behind(second, start) + step1.astype(F32)).astype(BF), middle)
        white_a = (third + step1.astype(F32) + jnp.where(top, 0.0, step2.astype(F32)) + start).astype(BF)
        moved4 = factor_x(behind(own4, start))
        t_a, p_a = white_a[:count_t], white_a[count_t:]
        t_moved_a = [inner(t_a, s, 0) for s in range(1, nx)]
        p_moved_a = [over_pool(p_a, s) for s in range(1, n_pool)]
        far4 = factor_flip(moved4)
        done = fence([step3, step4], [*t_moved_a, *p_moved_a], far4)

        fourth = partial([own4] + moved4 + [flip4] + far4)
        t_moved_a = [behind(v, done) for v in t_moved_a]
        t_flip_a = inner(behind(t_a, done), 0, 1)
        white_b = (jnp.where(top, fourth, second + step3.astype(F32) + step4.astype(F32)) + done).astype(BF)
        t_b, p_b = white_b[:count_t], white_b[count_t:]
        t_moved_b = [inner(t_b, s, 0) for s in range(1, nx)]
        p_moved_b = [over_pool(p_b, s) for s in range(1, n_pool)]
        t_flip_b = inner(t_b, 0, 1)

        def groups(t, t_moved, t_flip):
            far, far_flip = jnp.concatenate(t_moved, axis=0), jnp.concatenate([inner(v, 0, 1) for v in t_moved], axis=0)
            keep = jnp.where(top, t_flip, t), jnp.where(top, far_flip, far)
            give = jnp.where(top, t, t_flip), jnp.where(top, far, far_flip)
            return keep, give

        keep_a, give_a = groups(t_a, t_moved_a, t_flip_a)
        keep_b, give_b = groups(t_b, t_moved_b, t_flip_b)
        p_far_a, p_far_b = jnp.concatenate(p_moved_a, axis=0), jnp.concatenate(p_moved_b, axis=0)
        p_all_a, p_all_b = jnp.concatenate([p_a, p_far_a], axis=0), jnp.concatenate([p_b, p_far_b], axis=0)

        given_near = along_z(matmul_t(give_a[0], p_a) + matmul_t(give_b[0], p_b), owners)
        swapped = token(given_near)
        swapped = swapped if p_far_a.shape[0] == p_a.shape[0] else swapped[:, :1]
        give_side = behind(matmul_t(give_a[0], p_far_a) + matmul_t(give_b[0], p_far_b), swapped)
        given_side = along_z(give_side, owners)
        given_far = along_z(matmul_t(give_a[1], p_all_a) + matmul_t(give_b[1], p_all_b), owners)

        p_squares = square_sum(p_all_a) + square_sum(p_all_b)
        sizes = [p_squares.shape[0], keep_a[0].shape[0], keep_a[1].shape[0]]
        squares = along_z(jnp.concatenate(
            [p_squares] + [square_sum(a) + square_sum(b) for a, b in zip(give_a, give_b)]
        ), owners)
        pool_var = 1.0 + (p_squares + squares[:sizes[0]])

        hold = token(given_side)[:, :1]

        def log_sums(group, given, offset):
            a, b = behind(keep_a[group], hold), behind(keep_b[group], hold)
            target_var = 1.0 + (square_sum(a) + square_sum(b) + squares[offset:offset + sizes[1 + group]])
            cross = matmul_t(a, p_all_a) + matmul_t(b, p_all_b) + given
            ratio = jnp.square(cross) / (target_var[:, None] * pool_var[None, :])
            return -0.5 * jnp.sum(jnp.log1p(-ratio), axis=0)

        sums = log_sums(0, jnp.concatenate([given_near, given_side], axis=1), sizes[0])
        sums = sums + log_sums(1, given_far, sizes[0] + sizes[1])

        blocks = [sums[s * count:(s + 1) * count] for s in range(n_pool)]
        own = blocks[0] + along_z(blocks[0], owners)
        for s in range(1, n_pool):
            own = own + (over_pool(blocks[s], -s) + over_pool(blocks[s], -s, 0, owners))
        rows = [in_order([own if s == 0 else inner(own, s, 0), inner(own, s, 1)], core) for s in range(nx)]
        scores = in_order(rows, x)
        return jnp.where(z >= nz - 2, scores, along_z(scores, skip))

    return body


def solution(mesh):
    in_specs = (P("pool", "tgt"), P("pool"), P("pool", "tgt"), P("tgt", None))
    out_specs = P("pool")
    body = make_body(mesh.shape["pool"], mesh.shape["tgt"])
    return jax.shard_map(body, mesh=mesh, in_specs=in_specs, out_specs=out_specs, check_vma=False)
```
